32 devices in a mesh: row: 4 (over z), col: 8 (over y, x, core).
Axes of the slice: x: 2, y: 2, z: 4, core: 2. Of those that a mesh axis runs over, the one named last changes fastest.
Arguments:
- t2_amps: bfloat16 [8192, 2048], P('row', 'col'), may hold values from -6 to 6
- v_ints: bfloat16 [2048, 16384], P('row', 'col'), may hold values from -0.125 to 0.125
- t2_mask: int32 [64, 16], P('row', 'col'), may hold values 0 or 1
- v_mask: int32 [16, 128], P('row', 'col'), may hold values 0 or 1
Outputs:
- ladder: bfloat16 [8192, 16384], P('row', 'col')
The draws below stay inside these ranges and needn't reach their ends.
All inputs are finite; a program needn't handle non-finite values. No bound on the sum of `t2_mask` or of `v_mask` on one device may be relied on, other than what follows from the above.
Results may differ from the reference program's by a relative error of at most 0.001.
Values may be sent and summed in bfloat16 or wider, within the bound.
No kernel may reach another device: no remote copies, remote signals or barrier semaphores. Data moves between devices by JAX's collectives and lax.ppermute only.
A program may use at most 64 MiB of HBM per device.

```python
import jax
import jax.numpy as jnp
from jax import lax

TILE = 128
CD_TILES = 16
IJ_DEV = 2048
CD = 2048
IJ = 8192
AB = 16384
N_ROW = 4


def plant(entries, rng, low, largest):
    longest = entries.shape.index(max(entries.shape))
    spots = []
    for shift in (0, 1):
        where = [jax.random.randint(jax.random.fold_in(rng, axis), (), 0, length) for axis, length in enumerate(entries.shape)]
        where[longest] = (where[longest] + shift) % entries.shape[longest]
        spots.append(tuple(where))
    return entries.at[spots[0]].set(low).at[spots[1]].set(largest)


def level_of(stream_key, dims, pieces, least, top_value):
    loudness = 1.0
    for dim, blocks in pieces:
        draws = jax.random.uniform(jax.random.fold_in(jax.random.fold_in(stream_key, 6), dim), (blocks,), jnp.float32, least / len(pieces), top_value / len(pieces))
        loudness = loudness * jnp.repeat(jnp.exp(draws), dims[dim] // blocks).reshape((-1,) + (1,) * (len(dims) - 1 - dim))
    return loudness


def noise(rng, extent, deviation, reach, cuts=(), held_as=jnp.bfloat16):
    result = deviation * jax.random.normal(rng, extent, jnp.float32)
    if cuts:
        result = result * level_of(rng, extent, cuts, -0.22, 0.18)
    return jnp.clip(result, -reach, reach).astype(held_as)


def setup_inputs(seed: int = 0) -> dict:
    key_of = jax.random.split(jax.random.key(seed), 5)
    t2_amps = noise(key_of[0], (IJ, CD), 1.0, 6.0, ((0, 4), (1, 8)))
    v_ints = noise(key_of[1], (CD, AB), CD ** -0.5, 0.125, ((0, 4), (1, 8)))
    t2_mask = plant((jax.random.randint(key_of[2], (IJ // TILE, CD_TILES), 0, 4) < 3).astype(jnp.int32), jax.random.fold_in(key_of[2], 1), 0, 1)
    v_mask = plant((jax.random.randint(key_of[3], (CD_TILES, AB // TILE), 0, 4) < 3).astype(jnp.int32), jax.random.fold_in(key_of[3], 1), 0, 1)
    return dict(t2_amps=t2_amps, v_ints=v_ints, t2_mask=t2_mask, v_mask=v_mask)


def expand(mask, rows, cols):
    kept = jnp.broadcast_to(mask[:, None, :, None] > 0, (mask.shape[0], TILE, mask.shape[1], TILE))
    return kept.reshape(rows, cols)


def reference(t2_amps, v_ints, t2_mask, v_mask):
    masked_t2 = jnp.where(expand(t2_mask, IJ, CD), t2_amps, jnp.zeros_like(t2_amps))
    masked_v = jnp.where(expand(v_mask, CD, AB), v_ints, jnp.zeros_like(v_ints))
    blocks = masked_t2.reshape(N_ROW, IJ_DEV, CD)

    def one_block(block):
        return jnp.dot(block, masked_v, preferred_element_type=jnp.float32).astype(jnp.bfloat16)

    ladder = lax.map(one_block, blocks)
    return ladder.reshape(IJ, AB)
```

```python
import functools

import jax
import jax.numpy as jnp
from jax import lax
from jax.experimental import pallas as pl
from jax.experimental.pallas import tpu as pltpu
from jax.sharding import PartitionSpec as P

TILE = 128
PAIR = 2 * TILE
BF16 = jnp.bfloat16
SMEM = pl.BlockSpec(memory_space=pltpu.SMEM)
VMEM = pl.BlockSpec(memory_space=pltpu.VMEM)
ANY = pl.BlockSpec(memory_space=pl.ANY)
PARAMS = pltpu.CompilerParams(vmem_limit_bytes=48 << 20)
LENGTHS = (16, 20, 24, 28, 36)


def rows(tile, count=1):
    return pl.ds(pl.multiple_of(tile * TILE, TILE), count * TILE)


def tiles(count):
    return jax.ShapeDtypeStruct((count * TILE, TILE), BF16)


class Sizes:
    def __init__(self, n, k_tiles, n_tiles):
        self.n, self.kd, self.nd = n, k_tiles, n_tiles
        self.all = k_tiles * n_tiles
        self.half = self.all * 11 // 32
        self.main = 2 * self.half
        self.left = self.all - self.main
        self.stream = (n - 1) * self.left
        self.pairs = n_tiles // 2
        self.sure = (self.main // k_tiles) // 2
        lengths = {-(-f * self.stream // 60) for f in LENGTHS if f * self.stream // 60 > 0}
        self.lengths = sorted(lengths | {self.stream})


def pack_kernel(sz, mask, v, c0, c1, lf, packed):
    pos = jnp.int32(0)
    for c in range(sz.nd):
        for k in range(sz.kd):
            packed[rows(pos), :] = v[k * TILE : (k + 1) * TILE, c * TILE : (c + 1) * TILE]
            pos = pos + (mask[k, c] > 0).astype(jnp.int32)
    h = sz.half * TILE
    c0[...] = packed[:h, :]
    c1[...] = packed[h : 2 * h, :]
    lf[...] = packed[2 * h :, :]


def pack(sz, v, mask):
    return pl.pallas_call(
        functools.partial(pack_kernel, sz),
        out_shape=(tiles(sz.half), tiles(sz.half), tiles(sz.left)),
        in_specs=[SMEM, VMEM],
        out_specs=(VMEM, VMEM, VMEM),
        scratch_shapes=[pltpu.VMEM((sz.all * TILE, TILE), BF16)],
        compiler_params=PARAMS,
        name="pack",
    )(mask, v)


def screen_kernel(mask, t2, after, out):
    for i in range(mask.shape[0]):
        for k in range(mask.shape[1]):
            at = (slice(i * TILE, (i + 1) * TILE), slice(k * TILE, (k + 1) * TILE))
            tile = t2[at]
            out[at] = jnp.where(mask[i, k] > 0, tile, jnp.zeros_like(tile))


def screen(t2, mask, after):
    return pl.pallas_call(
        screen_kernel,
        out_shape=jax.ShapeDtypeStruct(t2.shape, BF16),
        in_specs=[SMEM, VMEM, ANY],
        out_specs=VMEM,
        compiler_params=PARAMS,
        name="screen",
    )(mask, t2, after)


def plan_kernel(sz, me_ref, masks, pos, info):
    me = me_ref[0]

    def column(c, carry):
        counts, firsts = list(carry[: sz.n]), list(carry[sz.n :])
        for z in range(sz.n):
            for k in range(sz.kd):
                kept = masks[z * sz.kd + k, c] > 0
                pos[z, c * sz.kd + k] = jnp.where(kept, counts[z], -1)
                late = jnp.logical_and(kept, counts[z] >= sz.main)
                firsts[z] = jnp.where(late, jnp.minimum(firsts[z], c), firsts[z])
                counts[z] = counts[z] + kept.astype(jnp.int32)
        return tuple(counts) + tuple(firsts)

    start = (jnp.int32(0),) * sz.n + (jnp.int32(sz.nd),) * sz.n
    out = lax.fori_loop(0, sz.nd, column, start)
    lefts = [jnp.maximum(c - sz.main, 0) for c in out[: sz.n]]
    whole = jnp.int32(sz.pairs - 1)
    for z in range(sz.n):
        whole = jnp.where(me == z, whole, jnp.minimum(whole, out[sz.n + z] // 2))
    info[0] = me
    info[1] = whole
    info[2] = jnp.maximum(sum(lefts[1:]), sum(lefts[:-1]))
    for z in range(sz.n):
        info[3 + z] = lefts[z]


def plan(sz, me, masks):
    return pl.pallas_call(
        functools.partial(plan_kernel, sz),
        out_shape=(
            jax.ShapeDtypeStruct((sz.n, sz.all), jnp.int32),
            jax.ShapeDtypeStruct((3 + sz.n,), jnp.int32),
        ),
        in_specs=[SMEM, SMEM],
        out_specs=(SMEM, SMEM),
        name="plan",
    )(me, masks)


def pool_kernel(sz, length, info, lf, *refs):
    q_up, q_down = refs[: sz.n - 2], refs[sz.n - 2 : 2 * (sz.n - 2)]
    out_up, out_down, joined = refs[2 * (sz.n - 2) :]
    me = info[0]
    for end, step, q, out in ((sz.n - 1, -1, q_up, out_up), (0, 1, q_down, out_down)):
        source = end + step

        @pl.when(me == source)
        def _():
            at = jnp.int32(0)
            for s, part in enumerate((lf,) + tuple(q)):
                joined[rows(at, sz.left), :] = part[...]
                at = at + info[3 + source + s * step]
            out[...] = joined[: length * TILE, :]


def pool(sz, length, info, lf, q_up, q_down):
    return pl.pallas_call(
        functools.partial(pool_kernel, sz, length),
        out_shape=(tiles(length), tiles(length)),
        in_specs=[SMEM] + [VMEM] * (1 + 2 * (sz.n - 2)),
        out_specs=(VMEM, VMEM),
        scratch_shapes=[pltpu.VMEM((sz.stream * TILE, TILE), BF16)],
        compiler_params=PARAMS,
        name="pool",
    )(info, lf, *q_up, *q_down)


def t2_copies(t2, t2_v, sem):
    half = t2_v.shape[0] // 2
    return [
        pltpu.make_async_copy(
            t2.at[pl.ds(r * half, half), :], t2_v.at[pl.ds(r * half, half), :], sem.at[r]
        )
        for r in range(2)
    ]


def out_copy(out, held, sem, slot, r, pair):
    half = held.shape[1] // 2
    return pltpu.make_async_copy(
        held.at[slot, pl.ds(r * half, half), :],
        out.at[pl.ds(r * half, half), pl.ds(pl.multiple_of(pair * PAIR, PAIR), PAIR)],
        sem.at[slot, r],
    )


def multiply(t2_v, b, out, held, sem, pair, step):
    half = held.shape[1] // 2
    slot = lax.rem(step, 2)
    for r in range(2):

        @pl.when(step >= 2)
        def _():
            out_copy(out, held, sem, slot, r, pair).wait()

        held[slot, pl.ds(r * half, half), :] = jnp.dot(
            t2_v[pl.ds(r * half, half), :], b[...], preferred_element_type=jnp.float32
        ).astype(BF16)
        out_copy(out, held, sem, slot, r, pair).start()


def drain(out, held, sem, steps):
    for back in (1, 2):

        @pl.when(steps >= back)
        def _():
            for r in range(2):
                out_copy(out, held, sem, lax.rem(steps - back, 2), r, 0).wait()


def main_kernel(sz, info, pos, t2, *refs):
    n, h = sz.n, sz.half
    own, lf = refs[:2], refs[2]
    up, down = refs[3 : 3 + 2 * (n - 1)], refs[3 + 2 * (n - 1) : 3 + 4 * (n - 1)]
    out, rest = refs[3 + 4 * (n - 1) : 5 + 4 * (n - 1)]
    t2_v, packed, b, held, t2_sem, in_sem, out_sem, rest_sem = refs[5 + 4 * (n - 1) :]
    me, whole = info[0], info[1]
    for m in range(n):

        @pl.when(me == m)
        def _():
            for z in range(n):
                for c in range(2):
                    if z == m:
                        source = own[c]
                    elif z < m:
                        source = up[2 * (m - z - 1) + c]
                    else:
                        source = down[2 * (z - m - 1) + c]
                    pltpu.make_async_copy(
                        source, packed.at[z, pl.ds(c * h * TILE, h * TILE), :], in_sem.at[z, c]
                    ).start()

    left = pl.ds(sz.main * TILE, sz.left * TILE)
    pltpu.make_async_copy(lf, packed.at[me, left, :], in_sem.at[0, 2]).start()
    for copy in t2_copies(t2, t2_v, t2_sem):
        copy.start()
    for z in range(n):
        for c in range(2):
            pltpu.make_async_copy(
                own[c], packed.at[z, pl.ds(c * h * TILE, h * TILE), :], in_sem.at[z, c]
            ).wait()
    pltpu.make_async_copy(lf, packed.at[me, left, :], in_sem.at[0, 2]).wait()

    def build(dst, pair):
        for z in range(n):
            here = jnp.where(me == z, sz.all, sz.main)
            for c in range(2):
                for k in range(sz.kd):
                    p = pos[z, (2 * pair + c) * sz.kd + k]
                    valid = jnp.logical_and(p >= 0, p < here)
                    tile = packed[z, rows(jnp.maximum(p, 0)), :]
                    at = (z * sz.kd + k) * TILE
                    dst[at : at + TILE, c * TILE : (c + 1) * TILE] = jnp.where(
                        valid, tile, jnp.zeros_like(tile)
                    )

    def rest_copy(j):
        return pltpu.make_async_copy(b.at[1 + j], rest.at[j], rest_sem.at[j])

    for j in range(sz.pairs - sz.sure):
        build(b.at[1 + j], sz.sure + j)
        rest_copy(j).start()
    for copy in t2_copies(t2, t2_v, t2_sem):
        copy.wait()

    @pl.loop(0, whole)
    def _(pair):
        build(b.at[0], pair)
        multiply(t2_v, b.at[0], out, held, out_sem, pair, pair)

    drain(out, held, out_sem, whole)
    for j in range(sz.pairs - sz.sure):
        rest_copy(j).wait()


def main_part(sz, info, pos, t2, own, lf, up, down):
    ij, cd = t2.shape
    ops = (*own, lf, *up, *down)
    late = sz.pairs - sz.sure
    return pl.pallas_call(
        functools.partial(main_kernel, sz),
        out_shape=(
            jax.ShapeDtypeStruct((ij, sz.nd * TILE), BF16),
            jax.ShapeDtypeStruct((late, cd, PAIR), BF16),
        ),
        in_specs=[SMEM, SMEM, ANY] + [ANY] * len(ops),
        out_specs=(ANY, ANY),
        scratch_shapes=[
            pltpu.VMEM((ij, cd), BF16),
            pltpu.VMEM((sz.n, sz.all * TILE, TILE), BF16),
            pltpu.VMEM((1 + late, cd, PAIR), BF16),
            pltpu.VMEM((2, ij, PAIR), BF16),
            pltpu.SemaphoreType.DMA((2,)),
            pltpu.SemaphoreType.DMA((sz.n, 3)),
            pltpu.SemaphoreType.DMA((2, 2)),
            pltpu.SemaphoreType.DMA((late,)),
        ],
        compiler_params=PARAMS,
        cost_estimate=pl.CostEstimate(
            flops=2 * ij * cd * sz.nd * TILE * 3 // 4, bytes_accessed=30 << 20, transcendentals=0
        ),
        name="main_part",
    )(info, pos, t2, *ops)


def tail_kernel(sz, info, pos, t2, begun, rest, *refs):
    n = sz.n
    end_up, end_down = refs[:2]
    q_up, q_down = refs[2:n], refs[n : 2 * n - 2]
    out, t2_v, b, extra, held, t2_sem, b_sem, in_sem, out_sem = refs[2 * n - 2 :]
    me, whole = info[0], info[1]
    length = end_up.shape[0]
    region = extra.shape[1]

    def copies(is_end, side, end, q):
        if is_end:
            return [pltpu.make_async_copy(end, extra.at[side, pl.ds(0, length), :], in_sem.at[side, 0])]
        size = sz.left * TILE
        return [
            pltpu.make_async_copy(part, extra.at[side, pl.ds(s * size, size), :], in_sem.at[side, s])
            for s, part in enumerate(q)
        ]

    sides = ((0, n - 1, end_up, q_up), (1, 0, end_down, q_down))

    def each(act):
        for side, last, end, q in sides:
            for is_end in (True, False):

                @pl.when((me == last) if is_end else (me != last))
                def _():
                    for copy in copies(is_end, side, end, q):
                        act(copy)

    each(lambda copy: copy.start())
    rest_copies = [
        pltpu.make_async_copy(rest.at[j], b.at[j], b_sem.at[j]) for j in range(sz.pairs - sz.sure)
    ]
    for copy in rest_copies:
        copy.start()
    for copy in t2_copies(t2, t2_v, t2_sem):
        copy.start()
    each(lambda copy: copy.wait())
    for copy in rest_copies:
        copy.wait()

    bases = []
    for z in range(n):
        base = jnp.int32(0)
        up_end = sum((info[3 + y] for y in range(z + 1, n - 1)), jnp.int32(0))
        down_end = sum((info[3 + y] for y in range(1, z)), jnp.int32(0))
        base = jnp.where(z < me, jnp.where(me == n - 1, up_end, (me - z - 1) * sz.left), base)
        base = jnp.where(z > me, jnp.where(me == 0, down_end, (z - me - 1) * sz.left), base)
        bases.append(base)

    for j in range(sz.pairs - sz.sure):
        for z in range(n):
            side = (z > me).astype(jnp.int32)
            for c in range(2):
                for k in range(sz.kd):
                    p = pos[z, (2 * (sz.sure + j) + c) * sz.kd + k]

                    @pl.when(jnp.logical_and(p >= sz.main, me != z))
                    def _():
                        at = (z * sz.kd + k) * TILE
                        b[j, at : at + TILE, c * TILE : (c + 1) * TILE] = extra[
                            side, rows(bases[z] + p - sz.main), :
                        ]

    for copy in t2_copies(t2, t2_v, t2_sem):
        copy.wait()

    @pl.loop(whole, sz.pairs)
    def _(pair):
        multiply(t2_v, b.at[pair - sz.sure], out, held, out_sem, pair, pair - whole)

    drain(out, held, out_sem, sz.pairs - whole)


def tail_part(sz, info, pos, t2, begun, rest, ends, q_up, q_down):
    ij, cd = t2.shape
    late = sz.pairs - sz.sure
    ops = (*ends, *q_up, *q_down)
    region = max(ends[0].shape[0], (sz.n - 2) * sz.left * TILE)
    return pl.pallas_call(
        functools.partial(tail_kernel, sz),
        out_shape=jax.ShapeDtypeStruct(begun.shape, BF16),
        in_specs=[SMEM, SMEM, ANY, ANY, ANY] + [ANY] * len(ops),
        out_specs=ANY,
        scratch_shapes=[
            pltpu.VMEM((ij, cd), BF16),
            pltpu.VMEM((late, cd, PAIR), BF16),
            pltpu.VMEM((2, region, TILE), BF16),
            pltpu.VMEM((2, ij, PAIR), BF16),
            pltpu.SemaphoreType.DMA((2,)),
            pltpu.SemaphoreType.DMA((late,)),
            pltpu.SemaphoreType.DMA((2, max(1, sz.n - 2))),
            pltpu.SemaphoreType.DMA((2, 2)),
        ],
        input_output_aliases={3: 0},
        compiler_params=PARAMS,
        cost_estimate=pl.CostEstimate(
            flops=2 * ij * cd * sz.nd * TILE // 4, bytes_accessed=16 << 20, transcendentals=0
        ),
        name="tail_part",
    )(info, pos, t2, begun, rest, *ops)


def last_hop(sz, length, info, pos, t2, own, lf, up, down, q_up, q_down):
    n = sz.n
    to_up, to_down = pool(sz, length, info, lf, q_up, q_down)
    end_up = lax.ppermute(to_up, "row", [(n - 2, n - 1)])
    end_down = lax.ppermute(to_down, "row", [(1, 0)])
    begun, rest = main_part(sz, info, pos, t2, own, lf, up, down)
    return tail_part(sz, info, pos, t2, begun, rest, (end_up, end_down), q_up, q_down)


def body(n, t2_amps, v_ints, t2_mask, v_mask):
    sz = Sizes(n, *v_mask.shape)
    me = lax.axis_index("row")
    c0, c1, lf = pack(sz, v_ints, v_mask)
    t2 = lax.all_gather(screen(t2_amps, t2_mask, c0), "col", axis=1, tiled=True)

    hops = [[(i, i + 1) for i in range(s, n - 1)] for s in range(n - 1)]
    back = [[(n - 1 - a, n - 1 - b) for a, b in hop] for hop in hops]
    up, down = [], []
    at_up, at_down = [c0, c1], [c0, c1]
    for s in range(n - 1):
        for c in range(2):
            at_up[c] = lax.ppermute(at_up[c], "row", hops[s])
            at_down[c] = lax.ppermute(at_down[c], "row", back[s])
        up += at_up
        down += at_down
    q_up, q_down = [], []
    far_up, _ = lax.optimization_barrier((lf, up[1]))
    far_down, _ = lax.optimization_barrier((lf, down[1]))
    for s in range(n - 2):
        far_up = lax.ppermute(far_up, "row", hops[s][:-1])
        far_down = lax.ppermute(far_down, "row", back[s][:-1])
        q_up.append(far_up)
        q_down.append(far_down)

    spread = jnp.where(
        lax.broadcasted_iota(jnp.int32, (n, 1, 1), 0) == me, v_mask[None], jnp.zeros_like(v_mask[None])
    ).reshape(n * sz.kd, sz.nd)
    spread, _ = lax.optimization_barrier((spread, up[0]))
    masks = lax.psum(spread, "row")
    pos, info = plan(sz, me.reshape(1), masks)
    need = lax.pmax(info[2], "col")
    branch = sum((need > length).astype(jnp.int32) for length in sz.lengths[:-1])
    return lax.switch(
        branch,
        [functools.partial(last_hop, sz, length) for length in sz.lengths],
        info, pos, t2, (c0, c1), lf, up, down, q_up, q_down,
    )


def solution(mesh):
    in_specs = (P("row", "col"), P("row", "col"), P("row", "col"), P("row", "col"))
    return jax.shard_map(
        functools.partial(body, mesh.shape["row"]),
        mesh=mesh,
        in_specs=in_specs,
        out_specs=P("row", "col"),
        check_vma=False,
    )
```

```python
import functools

import jax
import jax.numpy as jnp
from jax import lax
from jax.experimental import pallas as pl
from jax.experimental.pallas import tpu as pltpu
from jax.sharding import PartitionSpec as P

TILE = 128
PAIR = 2 * TILE
BF16 = jnp.bfloat16
SMEM = pl.BlockSpec(memory_space=pltpu.SMEM)
VMEM = pl.BlockSpec(memory_space=pltpu.VMEM)
ANY = pl.BlockSpec(memory_space=pl.ANY)
PARAMS = pltpu.CompilerParams(vmem_limit_bytes=48 << 20)
LENGTHS = (8, 10, 12, 14, 16, 20)


def rows(tile, count=1):
    return pl.ds(pl.multiple_of(tile * TILE, TILE), count * TILE)


def tiles(count):
    return jax.ShapeDtypeStruct((count * TILE, TILE), BF16)


class Sizes:
    def __init__(self, n, k_tiles, n_tiles):
        self.n, self.kd, self.nd = n, k_tiles, n_tiles
        self.all = k_tiles * n_tiles
        self.half = self.all * 3 // 8
        self.main = 2 * self.half
        self.left = self.all - self.main
        self.stream = (n - 1) * self.left
        self.pairs = n_tiles // 2
        self.sure = (self.main // k_tiles) // 2
        lengths = {-(-f * self.stream // 48) for f in LENGTHS}
        self.lengths = sorted(lengths | {self.stream})


def pack_kernel(sz, mask, v, c0, c1, lf, packed):
    pos = jnp.int32(0)
    for c in range(sz.nd):
        for k in range(sz.kd):
            packed[rows(pos), :] = v[k * TILE : (k + 1) * TILE, c * TILE : (c + 1) * TILE]
            pos = pos + (mask[k, c] > 0).astype(jnp.int32)
    h = sz.half * TILE
    c0[...] = packed[:h, :]
    c1[...] = packed[h : 2 * h, :]
    lf[...] = packed[2 * h :, :]


def pack(sz, v, mask):
    return pl.pallas_call(
        functools.partial(pack_kernel, sz),
        out_shape=(tiles(sz.half), tiles(sz.half), tiles(sz.left)),
        in_specs=[SMEM, VMEM],
        out_specs=(VMEM, VMEM, VMEM),
        scratch_shapes=[pltpu.VMEM((sz.all * TILE, TILE), BF16)],
        compiler_params=PARAMS,
        name="pack",
    )(mask, v)


def screen_kernel(mask, t2, after, out):
    for i in range(mask.shape[0]):
        for k in range(mask.shape[1]):
            at = (slice(i * TILE, (i + 1) * TILE), slice(k * TILE, (k + 1) * TILE))
            tile = t2[at]
            out[at] = jnp.where(mask[i, k] > 0, tile, jnp.zeros_like(tile))


def screen(t2, mask, after):
    return pl.pallas_call(
        screen_kernel,
        out_shape=jax.ShapeDtypeStruct(t2.shape, BF16),
        in_specs=[SMEM, VMEM, ANY],
        out_specs=VMEM,
        compiler_params=PARAMS,
        name="screen",
    )(mask, t2, after)


def plan_kernel(sz, me_ref, masks, place, late, info):
    n, me = sz.n, me_ref[0]

    def column(c, carry):
        counts, firsts, seconds = (list(carry[i * n : (i + 1) * n]) for i in range(3))
        for z in range(n):
            here = jnp.where(me == z, sz.all, sz.main)
            for k in range(sz.kd):
                i = c * n * sz.kd + z * sz.kd + k
                kept, p = masks[z * sz.kd + k, c] > 0, counts[z]
                place[i] = jnp.where(jnp.logical_and(kept, p < here), z * sz.all + p, n * sz.all)
                late[i] = jnp.where(jnp.logical_and(kept, p >= here), p - sz.main, -1)
                over = jnp.logical_and(kept, p >= sz.half)
                firsts[z] = jnp.where(over, jnp.minimum(firsts[z], c), firsts[z])
                over = jnp.logical_and(kept, p >= here)
                seconds[z] = jnp.where(over, jnp.minimum(seconds[z], c), seconds[z])
                counts[z] = p + kept.astype(jnp.int32)
        return tuple(counts + firsts + seconds)

    start = (jnp.int32(0),) * n + (jnp.int32(sz.nd),) * (2 * n)
    out = lax.fori_loop(0, sz.nd, column, start)
    lefts = [jnp.maximum(c - sz.main, 0) for c in out[:n]]
    info[0] = me
    info[1] = jnp.int32(0)
    info[2] = functools.reduce(jnp.minimum, out[n : 2 * n], jnp.int32(sz.nd - 2)) // 2
    info[3] = functools.reduce(jnp.minimum, out[2 * n :], jnp.int32(sz.nd - 2)) // 2
    info[4] = jnp.int32(sz.pairs)
    info[5] = jnp.maximum(sum(lefts[1:]), sum(lefts[:-1]))
    for z in range(n):
        info[6 + z] = lefts[z]


def plan(sz, me, masks):
    return pl.pallas_call(
        functools.partial(plan_kernel, sz),
        out_shape=(
            jax.ShapeDtypeStruct((sz.n * sz.all,), jnp.int32),
            jax.ShapeDtypeStruct((sz.n * sz.all,), jnp.int32),
            jax.ShapeDtypeStruct((6 + sz.n,), jnp.int32),
        ),
        in_specs=[SMEM, SMEM],
        out_specs=(SMEM, SMEM, SMEM),
        name="plan",
    )(me, masks)


def pool_kernel(sz, length, info, lf, *refs):
    q_up, q_down = refs[: sz.n - 2], refs[sz.n - 2 : 2 * (sz.n - 2)]
    out_up, out_down, joined = refs[2 * (sz.n - 2) :]
    me = info[0]
    for end, step, q, out in ((sz.n - 1, -1, q_up, out_up), (0, 1, q_down, out_down)):
        source = end + step

        @pl.when(me == source)
        def _():
            at = jnp.int32(0)
            for s, part in enumerate((lf,) + tuple(q)):
                joined[rows(at, sz.left), :] = part[...]
                at = at + info[6 + source + s * step]
            out[...] = joined[: length * TILE, :]


def pool(sz, length, info, lf, q_up, q_down):
    return pl.pallas_call(
        functools.partial(pool_kernel, sz, length),
        out_shape=(tiles(length), tiles(length)),
        in_specs=[SMEM] + [VMEM] * (1 + 2 * (sz.n - 2)),
        out_specs=(VMEM, VMEM),
        scratch_shapes=[pltpu.VMEM((sz.stream * TILE, TILE), BF16)],
        compiler_params=PARAMS,
        name="pool",
    )(info, lf, *q_up, *q_down)


def out_copy(out, held, sem, slot, pair):
    return pltpu.make_async_copy(
        held.at[slot], out.at[:, pl.ds(pl.multiple_of(pair * PAIR, PAIR), PAIR)], sem.at[slot]
    )


def multiply(lo, hi, build, t2_v, out, held, sem):
    half = held.shape[1] // 2

    @pl.loop(lo, hi)
    def _(pair):
        slot = lax.rem(pair, 2)
        b = build(pair)

        @pl.when(pair >= lo + 2)
        def _():
            out_copy(out, held, sem, slot, pair).wait()

        for r in range(2):
            at = slice(r * half, (r + 1) * half)
            held[slot, at, :] = jnp.dot(
                t2_v[at, :], b[...], preferred_element_type=jnp.float32
            ).astype(BF16)
        out_copy(out, held, sem, slot, pair).start()

    for back in (1, 2):

        @pl.when(hi - back >= lo)
        def _():
            out_copy(out, held, sem, lax.rem(hi - back, 2), 0).wait()


def main_kernel(sz, chunks, info, place, t2, *refs):
    n, h = sz.n, sz.half * TILE
    own, refs = refs[:chunks], refs[chunks:]
    if chunks == 2:
        lf, begun, *refs = refs
    up, refs = refs[: chunks * (n - 1)], refs[chunks * (n - 1) :]
    down, refs = refs[: chunks * (n - 1)], refs[chunks * (n - 1) :]
    if chunks == 2:
        out, rest, t2_v, packed, b, held, t2_sem, in_sem, out_sem, rest_sem = refs
    else:
        out, t2_v, packed, b, held, t2_sem, in_sem, out_sem = refs
    me = info[0]
    t2_copy = pltpu.make_async_copy(t2, t2_v, t2_sem)

    def chunk_copy(source, z, c):
        return pltpu.make_async_copy(
            source, packed.at[pl.ds(z * sz.all * TILE + c * h, h), :], in_sem.at[z, c]
        )

    for m in range(n):

        @pl.when(me == m)
        def _():
            for z in range(n):
                for c in range(chunks):
                    if z == m:
                        source = own[c]
                    elif z < m:
                        source = up[chunks * (m - z - 1) + c]
                    else:
                        source = down[chunks * (z - m - 1) + c]
                    chunk_copy(source, z, c).start()

    if chunks == 2:
        left_copy = pltpu.make_async_copy(
            lf, packed.at[rows(me * sz.all + sz.main, sz.left), :], in_sem.at[0, 2]
        )
        left_copy.start()
    t2_copy.start()
    packed[n * sz.all * TILE :, :] = jnp.zeros((TILE, TILE), BF16)
    for z in range(n):
        for c in range(chunks):
            chunk_copy(own[c], z, c).wait()
    if chunks == 2:
        left_copy.wait()

    def build(pair, to=0):
        @pl.loop(0, n * sz.kd)
        def _(k):
            for c in range(2):
                tile = packed[rows(place[(2 * pair + c) * n * sz.kd + k]), :]
                b[to, rows(k), c * TILE : (c + 1) * TILE] = tile

        return b.at[to]

    if chunks == 2:
        rest_copies = []
        for j in range(sz.pairs - sz.sure):
            build(sz.sure + j, 1 + j)
            rest_copies.append(pltpu.make_async_copy(b.at[1 + j], rest.at[j], rest_sem.at[j]))
            rest_copies[-1].start()
    t2_copy.wait()
    multiply(info[chunks], info[chunks + 1], build, t2_v, out, held, out_sem)
    if chunks == 2:
        for copy in rest_copies:
            copy.wait()


def main_part(sz, chunks, info, place, t2, own, up, down, lf=None, begun=None):
    ij, cd = t2.shape
    ops = list(own[:chunks])
    out_shape = [jax.ShapeDtypeStruct((ij, sz.nd * TILE), BF16)]
    late, aliases = 0, {}
    if chunks == 2:
        late, aliases = sz.pairs - sz.sure, {3 + len(ops) + 1: 0}
        ops += [lf, begun]
        out_shape.append(jax.ShapeDtypeStruct((late, cd, PAIR), BF16))
    for hop in up + down:
        ops += hop[:chunks]
    out = pl.pallas_call(
        functools.partial(main_kernel, sz, chunks),
        out_shape=out_shape,
        in_specs=[SMEM, SMEM, ANY] + [ANY] * len(ops),
        out_specs=[ANY] * len(out_shape),
        scratch_shapes=[
            pltpu.VMEM((ij, cd), BF16),
            pltpu.VMEM(((sz.n * sz.all + 1) * TILE, TILE), BF16),
            pltpu.VMEM((1 + late, cd, PAIR), BF16),
            pltpu.VMEM((2, ij, PAIR), BF16),
            pltpu.SemaphoreType.DMA,
            pltpu.SemaphoreType.DMA((sz.n, 3)),
            pltpu.SemaphoreType.DMA((2,)),
        ]
        + ([pltpu.SemaphoreType.DMA((late,))] if late else []),
        input_output_aliases=aliases,
        compiler_params=PARAMS,
        cost_estimate=pl.CostEstimate(
            flops=ij * cd * sz.nd * TILE, bytes_accessed=20 << 20, transcendentals=0
        ),
        name="main_part",
    )(info, place, t2, *ops)
    return out if chunks == 2 else out[0]


def tail_kernel(sz, info, late, t2, begun, rest, *refs):
    n = sz.n
    end_up, end_down = refs[:2]
    q_up, q_down = refs[2:n], refs[n : 2 * n - 2]
    out, t2_v, b, extra, held, t2_sem, b_sem, in_sem, out_sem = refs[2 * n - 2 :]
    me = info[0]
    length = end_up.shape[0]
    region = extra.shape[0] // TILE // 2

    def copies(is_end, side, end, q):
        if is_end:
            parts, size = (end,), length
        else:
            parts, size = q, sz.left * TILE
        return [
            pltpu.make_async_copy(
                part, extra.at[pl.ds(side * region * TILE + s * size, size), :], in_sem.at[side, s]
            )
            for s, part in enumerate(parts)
        ]

    sides = ((0, n - 1, end_up, q_up), (1, 0, end_down, q_down))

    def each(act):
        for side, last, end, q in sides:
            for is_end in (True, False):

                @pl.when((me == last) if is_end else (me != last))
                def _():
                    for copy in copies(is_end, side, end, q):
                        act(copy)

    each(lambda copy: copy.start())
    rest_copies = [
        pltpu.make_async_copy(rest.at[j], b.at[j], b_sem.at[j]) for j in range(sz.pairs - sz.sure)
    ]
    for copy in rest_copies:
        copy.start()
    t2_copy = pltpu.make_async_copy(t2, t2_v, t2_sem)
    t2_copy.start()

    bases = []
    for z in range(n):
        up_end = sum((info[6 + y] for y in range(z + 1, n - 1)), jnp.int32(0))
        down_end = sum((info[6 + y] for y in range(1, z)), jnp.int32(0))
        above = jnp.where(me == n - 1, up_end, (me - z - 1) * sz.left)
        below = region + jnp.where(me == 0, down_end, (z - me - 1) * sz.left)
        bases.append(jnp.where(z < me, above, below))

    each(lambda copy: copy.wait())
    for copy in rest_copies:
        copy.wait()
    for j in range(sz.pairs - sz.sure):
        for z in range(n):

            @pl.loop(0, sz.kd)
            def _(k):
                for c in range(2):
                    p = late[((2 * (sz.sure + j) + c) * n + z) * sz.kd + k]

                    @pl.when(p >= 0)
                    def _():
                        b[j, rows(z * sz.kd + k), c * TILE : (c + 1) * TILE] = extra[
                            rows(bases[z] + p), :
                        ]

    t2_copy.wait()
    multiply(info[3], info[4], lambda pair: b.at[pair - sz.sure], t2_v, out, held, out_sem)


def tail_part(sz, info, late, t2, begun, rest, ends, q_up, q_down):
    ij, cd = t2.shape
    pairs = sz.pairs - sz.sure
    ops = (*ends, *q_up, *q_down)
    region = max(ends[0].shape[0], (sz.n - 2) * sz.left * TILE)
    return pl.pallas_call(
        functools.partial(tail_kernel, sz),
        out_shape=jax.ShapeDtypeStruct(begun.shape, BF16),
        in_specs=[SMEM, SMEM, ANY, ANY, ANY] + [ANY] * len(ops),
        out_specs=ANY,
        scratch_shapes=[
            pltpu.VMEM((ij, cd), BF16),
            pltpu.VMEM((pairs, cd, PAIR), BF16),
            pltpu.VMEM((2 * region, TILE), BF16),
            pltpu.VMEM((2, ij, PAIR), BF16),
            pltpu.SemaphoreType.DMA,
            pltpu.SemaphoreType.DMA((pairs,)),
            pltpu.SemaphoreType.DMA((2, max(1, sz.n - 2))),
            pltpu.SemaphoreType.DMA((2,)),
        ],
        input_output_aliases={3: 0},
        compiler_params=PARAMS,
        cost_estimate=pl.CostEstimate(
            flops=2 * ij * cd * pairs * PAIR, bytes_accessed=16 << 20, transcendentals=0
        ),
        name="tail_part",
    )(info, late, t2, begun, rest, *ops)


def last_hop(sz, length, info, place, late, t2, own, lf, up, down, q_up, q_down, begun):
    n = sz.n
    to_up, to_down = pool(sz, length, info, lf, q_up, q_down)
    end_up = lax.ppermute(to_up, "row", [(n - 2, n - 1)])
    end_down = lax.ppermute(to_down, "row", [(1, 0)])
    begun, rest = main_part(sz, 2, info, place, t2, own, up, down, lf, begun)
    return tail_part(sz, info, late, t2, begun, rest, (end_up, end_down), q_up, q_down)


def tie(value, after):
    return lax.optimization_barrier((value, after))[0]


def body(n, t2_amps, v_ints, t2_mask, v_mask):
    sz = Sizes(n, *v_mask.shape)
    me = lax.axis_index("row")
    *own, lf = pack(sz, v_ints, v_mask)

    hops = [[(i, i + 1) for i in range(s, n - 1)] for s in range(n - 1)]
    back = [[(n - 1 - a, n - 1 - b) for a, b in hop] for hop in hops]

    def hop(s, value, after=None):
        up, down = value
        if after is not None:
            up, down = tie(up, after), tie(down, after)
        return lax.ppermute(up, "row", hops[s]), lax.ppermute(down, "row", back[s])

    first = [hop(0, (own[0], own[0]))]
    second = [hop(0, (own[1], own[1]))]
    t2 = lax.all_gather(screen(t2_amps, t2_mask, first[0][0]), "col", axis=1, tiled=True)
    spread = jnp.where(
        lax.broadcasted_iota(jnp.int32, (n, 1, 1), 0) == me, v_mask[None], jnp.zeros_like(v_mask[None])
    ).reshape(n * sz.kd, sz.nd)
    masks = lax.psum(tie(spread, first[0][0]), "row")
    place, late, info = plan(sz, me.reshape(1), masks)
    need = None
    for s in range(1, n - 1):
        first.append(hop(s, first[-1]))
        second.append(hop(s, second[-1], masks if s == 1 else need))
        if need is None:
            need = lax.pmax(tie(info[5], first[-1][0]), "col")
    far = (tie(lf, second[0][0]), tie(lf, second[0][1]))
    q_up, q_down = [], []
    for s in range(n - 2):
        far = (
            lax.ppermute(far[0], "row", hops[s][:-1]),
            lax.ppermute(far[1], "row", back[s][:-1]),
        )
        q_up.append(far[0])
        q_down.append(far[1])
    up = [[a[0], b[0]] for a, b in zip(first, second)]
    down = [[a[1], b[1]] for a, b in zip(first, second)]
    begun = main_part(sz, 1, info, place, t2, own, up, down)

    branch = sum((need > length).astype(jnp.int32) for length in sz.lengths[:-1])
    return lax.switch(
        branch,
        [functools.partial(last_hop, sz, length) for length in sz.lengths],
        info, place, late, t2, own, lf, up, down, q_up, q_down, begun,
    )


def solution(mesh):
    in_specs = (P("row", "col"), P("row", "col"), P("row", "col"), P("row", "col"))
    return jax.shard_map(
        functools.partial(body, mesh.shape["row"]),
        mesh=mesh,
        in_specs=in_specs,
        out_specs=P("row", "col"),
        check_vma=False,
    )
```

```python
import functools

import jax
import jax.numpy as jnp
from jax import lax
from jax.experimental import pallas as pl
from jax.experimental.pallas import tpu as pltpu
from jax.sharding import PartitionSpec as P

TILE = 128
PAIR = 2 * TILE
NOTE = 16
BF16 = jnp.bfloat16
LEFTS = 6
SMEM = pl.BlockSpec(memory_space=pltpu.SMEM)
VMEM = pl.BlockSpec(memory_space=pltpu.VMEM)
ANY = pl.BlockSpec(memory_space=pl.ANY)
HBM = pl.BlockSpec(memory_space=pltpu.HBM)
PARAMS = pltpu.CompilerParams(vmem_limit_bytes=48 << 20)
COST = pl.CostEstimate(flops=1 << 20, bytes_accessed=1 << 12, transcendentals=0)
LENGTHS = (8, 10, 12, 14, 16, 20)
FIRST = 28


def rows(tile, count=1):
    return pl.ds(pl.multiple_of(tile * TILE, TILE), count * TILE)


def tiles(count):
    return jax.ShapeDtypeStruct((count * TILE, TILE), BF16)


class Sizes:
    def __init__(self, n, k_tiles, n_tiles):
        self.n, self.kd, self.nd = n, k_tiles, n_tiles
        self.all = k_tiles * n_tiles
        self.main = self.all * 3 // 4
        self.first = self.main * FIRST // 48
        self.left = self.all - self.main
        self.stream = (n - 1) * self.left
        self.pairs = n_tiles // 2
        self.sure = (self.main // k_tiles) // 2
        lengths = {-(-f * self.stream // 48) for f in LENGTHS}
        self.lengths = sorted(lengths | {self.stream})

    def cut(self, c):
        start, stop = ((0, self.first), (self.first, self.main))[c]
        begin = NOTE + start * TILE if c else 0
        return start, stop - start, pl.ds(begin, NOTE + stop * TILE - begin)


def begin_kernel(
    sz, mask_v, v_mask_hbm, t2_mask_hbm, v, t2, main, lf, t2_out,
    v_v, t2_v, packed, v_mask, t2_mask, note, v_sem, sem,
):
    group = sz.nd // v_sem.shape[0]
    copies = []
    for g in range(v_sem.shape[0]):
        at = pl.ds(g * group * TILE, group * TILE)
        copies.append(pltpu.make_async_copy(v.at[:, at], v_v.at[:, at], v_sem.at[g]))
    mask_copy = pltpu.make_async_copy(v_mask_hbm, v_mask, sem.at[0])
    t2_copies = (
        pltpu.make_async_copy(t2_mask_hbm, t2_mask, sem.at[1]),
        pltpu.make_async_copy(t2, t2_v, sem.at[2]),
    )
    for copy in (mask_copy, *copies, *t2_copies):
        copy.start()
    note[...] = jnp.zeros_like(note)
    note[: sz.kd, : sz.nd] = (mask_v[...] > 0).astype(jnp.int32)
    mask_copy.wait()
    pos = jnp.int32(0)
    for c in range(sz.nd):
        if c % group == 0:
            copies[c // group].wait()
        for k in range(sz.kd):
            packed[rows(pos), :] = v_v[k * TILE : (k + 1) * TILE, c * TILE : (c + 1) * TILE]
            pos = pos + (v_mask[k, c] > 0).astype(jnp.int32)
    main[:NOTE, :] = note[...].astype(BF16)
    main[NOTE:, :] = packed[: sz.main * TILE, :]
    lf[...] = packed[sz.main * TILE :, :]
    for copy in t2_copies:
        copy.wait()
    for k in range(t2_mask.shape[0]):
        for i in range(t2_mask.shape[1]):
            at = (slice(i * TILE, (i + 1) * TILE), slice(k * TILE, (k + 1) * TILE))
            tile = t2_v[at]
            t2_out[at] = jnp.where(t2_mask[k, i] > 0, tile, jnp.zeros_like(tile))


def begin(sz, v, t2, v_mask, t2_mask):
    groups = 4 if sz.nd % 4 == 0 else 1
    return pl.pallas_call(
        functools.partial(begin_kernel, sz),
        out_shape=(
            jax.ShapeDtypeStruct((NOTE + sz.main * TILE, TILE), BF16),
            tiles(sz.left),
            jax.ShapeDtypeStruct(t2.shape, BF16),
        ),
        in_specs=[VMEM, HBM, HBM, HBM, HBM],
        out_specs=(VMEM, VMEM, VMEM),
        scratch_shapes=[
            pltpu.VMEM(v.shape, BF16),
            pltpu.VMEM(t2.shape, BF16),
            pltpu.VMEM((sz.all * TILE, TILE), BF16),
            pltpu.SMEM(v_mask.shape, jnp.int32),
            pltpu.SMEM(t2_mask.shape[::-1], jnp.int32),
            pltpu.VMEM((NOTE, TILE), jnp.int32),
            pltpu.SemaphoreType.DMA((groups,)),
            pltpu.SemaphoreType.DMA((3,)),
        ],
        compiler_params=pltpu.CompilerParams(vmem_limit_bytes=60 << 20),
        name="begin",
    )(v_mask, v_mask, t2_mask.T, v, t2)


def need_kernel(sz, here, *refs):
    n = sz.n
    parts, (out, notes, sem) = refs[: 2 * n - 3], refs[2 * n - 3 :]
    copies = [
        pltpu.make_async_copy(ref.at[pl.ds(0, NOTE), :], notes.at[i], sem.at[i])
        for i, ref in enumerate(parts)
    ]
    for copy in copies:
        copy.start()
    for copy in copies:
        copy.wait()
    me = here[0]
    sources = [me]
    for s in range(n - 2):
        sources += [me - 1 - s, me + 1 + s]
    to_up = to_down = jnp.int32(0)
    for i, z in enumerate(sources):
        count = jnp.sum(notes[i].astype(jnp.float32)).astype(jnp.int32)
        left = jnp.where(jnp.logical_and(z >= 0, z < n), jnp.maximum(count - sz.main, 0), 0)
        to_up = to_up + jnp.where(z == n - 1, 0, left)
        to_down = to_down + jnp.where(z == 0, 0, left)
    out[0] = jnp.maximum(to_up, to_down)


def longest(sz, here, own, got):
    ops = (own, *(part for hop in got for part in hop))
    return pl.pallas_call(
        functools.partial(need_kernel, sz),
        out_shape=jax.ShapeDtypeStruct((1,), jnp.int32),
        in_specs=[SMEM] + [ANY] * len(ops),
        out_specs=SMEM,
        scratch_shapes=[
            pltpu.VMEM((len(ops), NOTE, TILE), BF16),
            pltpu.SemaphoreType.DMA((len(ops),)),
        ],
        name="longest",
    )(here, *ops)


def from_source(sz, me, own, got, act):
    for m in range(sz.n):

        @pl.when(me == m)
        def _():
            for z in range(sz.n):
                act(z, own if z == m else got[abs(z - m) - 1][0 if z < m else 1])


def plan_kernel(sz, here, *refs):
    n, me = sz.n, here[0]
    own, *parts, end = refs[: 2 * n - 2]
    place, late, info, notes, wide, masks, note_sem, mask_sem = refs[2 * n - 2 :]

    def note_copy(z, ref):
        at = ref.at[pl.ds(0, NOTE), :]
        return pltpu.make_async_copy(at, notes.at[pl.ds(z * NOTE, NOTE), :], note_sem.at[z])

    got = [parts[2 * s : 2 * s + 2] for s in range(n - 2)] + [(end, end)]
    from_source(sz, me, own, got, lambda z, ref: note_copy(z, ref).start())
    for z in range(n):
        note_copy(z, own).wait()
    wide[...] = notes[...].astype(jnp.int32)
    mask_copy = pltpu.make_async_copy(wide, masks, mask_sem)
    mask_copy.start()
    mask_copy.wait()

    def column(c, carry):
        counts, firsts, seconds = (list(carry[i * n : (i + 1) * n]) for i in range(3))
        for z in range(n):
            have = jnp.where(me == z, sz.all, sz.main)
            for k in range(sz.kd):
                i = c * n * sz.kd + z * sz.kd + k
                kept, p = masks[z * NOTE + k, c] > 0, counts[z]
                place[i] = jnp.where(jnp.logical_and(kept, p < have), z * sz.all + p, n * sz.all)
                late[i] = jnp.where(jnp.logical_and(kept, p >= have), p - sz.main, -1)
                over = jnp.logical_and(kept, p >= sz.first)
                firsts[z] = jnp.where(over, jnp.minimum(firsts[z], c), firsts[z])
                over = jnp.logical_and(kept, p >= have)
                seconds[z] = jnp.where(over, jnp.minimum(seconds[z], c), seconds[z])
                counts[z] = p + kept.astype(jnp.int32)
        return tuple(counts + firsts + seconds)

    start = (jnp.int32(0),) * n + (jnp.int32(sz.nd),) * (2 * n)
    out = lax.fori_loop(0, sz.nd, column, start)
    lefts = [jnp.maximum(c - sz.main, 0) for c in out[:n]]
    info[0] = me
    info[1] = jnp.int32(0)
    info[2] = functools.reduce(jnp.minimum, out[n : 2 * n], jnp.int32(sz.nd - 2)) // 2
    info[3] = functools.reduce(jnp.minimum, out[2 * n :], jnp.int32(sz.nd - 2)) // 2
    info[4] = jnp.int32(sz.pairs)
    info[5] = here[1]
    for z in range(n):
        info[LEFTS + z] = lefts[z]


def plan(sz, here, own, got, end):
    n, ops = sz.n, (own, *(part for hop in got for part in hop), end)
    return pl.pallas_call(
        functools.partial(plan_kernel, sz),
        out_shape=(
            jax.ShapeDtypeStruct((sz.n * sz.all,), jnp.int32),
            jax.ShapeDtypeStruct((sz.n * sz.all,), jnp.int32),
            jax.ShapeDtypeStruct((LEFTS + sz.n,), jnp.int32),
        ),
        in_specs=[SMEM] + [ANY] * len(ops),
        out_specs=(SMEM, SMEM, SMEM),
        scratch_shapes=[
            pltpu.VMEM((n * NOTE, TILE), BF16),
            pltpu.VMEM((n * NOTE, TILE), jnp.int32),
            pltpu.SMEM((n * NOTE, TILE), jnp.int32),
            pltpu.SemaphoreType.DMA((n,)),
            pltpu.SemaphoreType.DMA,
        ],
        name="plan",
    )(here, *ops)


def choose_kernel(sz, c, here, up, down, out, sem):
    at = sz.cut(c)[2]
    for mine, x in ((here[0] == sz.n - 2, up), (here[0] != sz.n - 2, down)):

        @pl.when(mine)
        def _():
            copy = pltpu.make_async_copy(x.at[at, :], out, sem)
            copy.start()
            copy.wait()


def choose(sz, c, here, up, down):
    return pl.pallas_call(
        functools.partial(choose_kernel, sz, c),
        out_shape=jax.ShapeDtypeStruct((sz.cut(c)[2].size, TILE), BF16),
        in_specs=[SMEM, ANY, ANY],
        out_specs=VMEM,
        scratch_shapes=[pltpu.SemaphoreType.DMA],
        compiler_params=PARAMS,
        name="choose",
    )(here, up, down)


def pool_kernel(sz, length, info, lf, *refs):
    n, me = sz.n, info[0]
    spread, (out, joined) = refs[: n - 1], refs[n - 1 :]
    for source, order in ((n - 2, range(n - 2, -1, -1)), (1, range(1, n))):

        @pl.when(me == source)
        def _():
            at = jnp.int32(0)
            for z in order:
                part = lf if z == source else spread[(z ^ source) - 1]
                joined[rows(at, sz.left), :] = part[...]
                at = at + info[LEFTS + z]
            out[...] = joined[: length * TILE, :]


def pool(sz, length, info, lf, spread):
    return pl.pallas_call(
        functools.partial(pool_kernel, sz, length),
        out_shape=tiles(length),
        in_specs=[SMEM] + [VMEM] * sz.n,
        out_specs=VMEM,
        scratch_shapes=[pltpu.VMEM((sz.stream * TILE, TILE), BF16)],
        compiler_params=PARAMS,
        name="pool",
    )(info, lf, *spread)


def out_copy(out, held, sem, slot, pair):
    return pltpu.make_async_copy(
        held.at[slot], out.at[:, pl.ds(pl.multiple_of(pair * PAIR, PAIR), PAIR)], sem.at[slot]
    )


def t2_copies(info, t2, t2_v, sem, r):
    half, wide = t2_v.shape[0] // 2, t2_v.shape[1] // len(t2)
    at = pl.ds(pl.multiple_of(r * half, half), half)
    for d, block in enumerate(t2):
        to = t2_v.at[at, pl.ds(pl.multiple_of((info[5] ^ d) * wide, wide), wide)]
        yield pltpu.make_async_copy(block.at[at, :], to, sem.at[d, r])


def multiply(lo, hi, build, info, t2, t2_v, t2_sem, out, held, sem):
    half = held.shape[1] // 2

    @pl.when(lo >= hi)
    def _():
        for r in range(2):
            for copy in t2_copies(info, t2, t2_v, t2_sem, r):
                copy.wait()

    @pl.loop(lo, hi)
    def _(pair):
        slot = lax.rem(pair - lo, 2)
        b = build(pair)

        @pl.when(pair >= lo + 2)
        def _():
            out_copy(out, held, sem, slot, pair).wait()

        @pl.loop(0, 2)
        def _(r):
            @pl.when(pair == lo)
            def _():
                for copy in t2_copies(info, t2, t2_v, t2_sem, r):
                    copy.wait()

            at = pl.ds(pl.multiple_of(r * half, half), half)
            held[slot, at, :] = jnp.dot(
                t2_v[at, :], b[...], preferred_element_type=jnp.float32
            ).astype(BF16)

        out_copy(out, held, sem, slot, pair).start()

    for back in (1, 2):

        @pl.when(hi - back >= lo)
        def _():
            out_copy(out, held, sem, lax.rem(hi - back - lo, 2), 0).wait()


def main_kernel(sz, chunks, n_t2, info, place, *refs):
    n = sz.n
    t2, refs = refs[:n_t2], refs[n_t2:]
    own, refs = refs[0], refs[1:]
    got, refs = [refs[2 * s : 2 * s + 2] for s in range(n - 2)], refs[2 * (n - 2) :]
    ends, refs = refs[:chunks], refs[chunks:]
    if chunks == 2:
        lf, begun, out, rest, packed, b, held, t2_v, in_sem, out_sem, t2_sem = refs
    else:
        out, packed, b, held, t2_v, in_sem, out_sem, t2_sem = refs
    me = info[0]

    def chunk_copy(ref, z, c):
        start, count, at = sz.cut(c)
        size = count * TILE
        first = at.start + at.size - size if ref.shape[0] > at.size else ref.shape[0] - size
        to = packed.at[pl.ds((z * sz.all + start) * TILE, size), :]
        return pltpu.make_async_copy(ref.at[pl.ds(first, size), :], to, in_sem.at[z, c])

    for c in range(chunks):
        parts = got + [(ends[c], ends[c])]
        from_source(sz, me, own, parts, lambda z, ref: chunk_copy(ref, z, c).start())
    if chunks == 2:
        left_copy = pltpu.make_async_copy(
            lf, packed.at[rows(me * sz.all + sz.main, sz.left), :], in_sem.at[0, 2]
        )
        left_copy.start()
    for r in range(2):
        for copy in t2_copies(info, t2, t2_v, t2_sem, r):
            copy.start()
    packed[n * sz.all * TILE :, :] = jnp.zeros((TILE, TILE), BF16)
    for z in range(n):
        for c in range(chunks):
            chunk_copy(own, z, c).wait()
    if chunks == 2:
        left_copy.wait()

    def build(pair, to=b):
        @pl.loop(0, n * sz.kd)
        def _(k):
            for c in range(2):
                tile = packed[rows(place[(2 * pair + c) * n * sz.kd + k]), :]
                to[rows(k), c * TILE : (c + 1) * TILE] = tile

        return to

    multiply(info[chunks], info[chunks + 1], build, info, t2, t2_v, t2_sem, out, held, out_sem)
    if chunks == 2:
        for j in range(sz.pairs - sz.sure):
            build(sz.sure + j, rest.at[j])


def main_part(sz, chunks, info, place, t2, own, got, ends, lf=None, begun=None):
    ij, cd = t2[0].shape[0], t2[0].shape[1] * len(t2)
    ops = [*t2, own, *(part for hop in got for part in hop), *ends[:chunks]]
    out_shape = [pltpu.HBM((ij, sz.nd * TILE), BF16)]
    aliases = {}
    if chunks == 2:
        ops += [lf, begun]
        aliases = {2 + len(ops) - 1: 0}
        out_shape.append(jax.ShapeDtypeStruct((sz.pairs - sz.sure, cd, PAIR), BF16))
    out = pl.pallas_call(
        functools.partial(main_kernel, sz, chunks, len(t2)),
        out_shape=out_shape,
        in_specs=[SMEM, SMEM] + [ANY] * len(ops),
        out_specs=[HBM, VMEM][:chunks],
        scratch_shapes=[
            pltpu.VMEM(((sz.n * sz.all + 1) * TILE, TILE), BF16),
            pltpu.VMEM((cd, PAIR), BF16),
            pltpu.VMEM((2, ij, PAIR), BF16),
            pltpu.VMEM((ij, cd), BF16),
            pltpu.SemaphoreType.DMA((sz.n, 3)),
            pltpu.SemaphoreType.DMA((2,)),
            pltpu.SemaphoreType.DMA((len(t2), 2)),
        ],
        input_output_aliases=aliases,
        compiler_params=PARAMS,
        cost_estimate=COST,
        name="main_part",
    )(info, place, *ops)
    return out if chunks == 2 else out[0]


def tail_kernel(sz, n_t2, info, late, begun, rest, *refs):
    n, me = sz.n, info[0]
    t2, (top_end, low_end, *refs) = refs[:n_t2], refs[n_t2:]
    spread, (out, b, extra, held, t2_v, in_sem, out_sem, t2_sem) = refs[: n - 1], refs[n - 1 :]
    is_end = jnp.logical_or(me == 0, me == n - 1)
    size = sz.left * TILE
    from_top, from_low = (
        [pltpu.make_async_copy(end, extra.at[pl.ds(0, end.shape[0]), :], in_sem.at[0])]
        for end in (top_end, low_end)
    )
    direct = [
        pltpu.make_async_copy(part, extra.at[pl.ds(i * size, size), :], in_sem.at[i])
        for i, part in enumerate(spread)
    ]

    def each(act):
        for which, copies in ((me == n - 1, from_top), (me == 0, from_low), (jnp.logical_not(is_end), direct)):

            @pl.when(which)
            def _():
                for copy in copies:
                    act(copy)

    each(lambda copy: copy.start())
    for r in range(2):
        for copy in t2_copies(info, t2, t2_v, t2_sem, r):
            copy.start()
    b[...] = rest[...]
    bases = []
    for z in range(n):
        top = sum((info[LEFTS + y] for y in range(z + 1, n - 1)), jnp.int32(0))
        bottom = sum((info[LEFTS + y] for y in range(1, z)), jnp.int32(0))
        base = jnp.where(is_end, jnp.where(me == 0, bottom, top), ((me ^ z) - 1) * sz.left)
        bases.append(base)

    each(lambda copy: copy.wait())
    for j in range(sz.pairs - sz.sure):
        for z in range(n):

            @pl.loop(0, sz.kd)
            def _(k):
                for c in range(2):
                    p = late[((2 * (sz.sure + j) + c) * n + z) * sz.kd + k]

                    @pl.when(p >= 0)
                    def _():
                        b[j, rows(z * sz.kd + k), c * TILE : (c + 1) * TILE] = extra[
                            rows(bases[z] + p), :
                        ]

    multiply(info[3], info[4], lambda pair: b.at[pair - sz.sure], info, t2, t2_v, t2_sem, out, held, out_sem)


def tail_part(sz, info, late, t2, begun, rest, ends, spread):
    ij, cd = t2[0].shape[0], t2[0].shape[1] * len(t2)
    pairs = sz.pairs - sz.sure
    region = max(ends[0].shape[0], (sz.n - 1) * sz.left * TILE)
    return pl.pallas_call(
        functools.partial(tail_kernel, sz, len(t2)),
        out_shape=pltpu.HBM(begun.shape, BF16),
        in_specs=[SMEM, SMEM, HBM, VMEM] + [ANY] * (len(t2) + sz.n + 1),
        out_specs=HBM,
        scratch_shapes=[
            pltpu.VMEM((pairs, cd, PAIR), BF16),
            pltpu.VMEM((region, TILE), BF16),
            pltpu.VMEM((2, ij, PAIR), BF16),
            pltpu.VMEM((ij, cd), BF16),
            pltpu.SemaphoreType.DMA((sz.n - 1,)),
            pltpu.SemaphoreType.DMA((2,)),
            pltpu.SemaphoreType.DMA((len(t2), 2)),
        ],
        input_output_aliases={2: 0},
        compiler_params=PARAMS,
        cost_estimate=COST,
        name="tail_part",
    )(info, late, begun, rest, *t2, *ends, *spread)


def last_hop(sz, length, info, place, late, t2, own, got, ends, lf, spread, begun):
    n = sz.n
    joined = pool(sz, length, info, lf, spread)
    came = [lax.ppermute(joined, "row", pair) for pair in ([(n - 2, n - 1)], [(1, 0)])]
    begun, rest = main_part(sz, 2, info, place, t2, own, got, ends, lf, begun)
    return tail_part(sz, info, late, t2, begun, rest, came, spread)


def tie(value, after):
    return lax.optimization_barrier((value, after))[0]


def body(n, n_col, t2_amps, v_ints, t2_mask, v_mask):
    sz = Sizes(n, *v_mask.shape)
    me = lax.axis_index("row")
    here = jnp.stack([me, lax.axis_index("col")])
    own, lf, screened = begin(sz, v_ints, t2_amps, v_mask, t2_mask)

    def hop(s, value, after=None):
        up, down = value
        if after is not None:
            up, down = tie(up, after), tie(down, after)
        pairs = [(i, i + 1) for i in range(s, n - 1)]
        back = [(n - 1 - i, n - 1 - j) for i, j in pairs]
        return lax.ppermute(up, "row", pairs), lax.ppermute(down, "row", back)

    def across(value, d):
        return lax.ppermute(value, "col", [(i, i ^ d) for i in range(n_col)])

    t2 = {0: screened}
    got = [hop(0, (own, own))]
    for d in range(2, n_col, 2):
        t2[d] = across(screened if d < 6 else tie(screened, t2[2]), d)
    for d in range(0, n_col, 2):
        t2[d + 1] = across(t2[d], 1)
    t2 = [t2[d] for d in range(n_col)]
    for s in range(1, n - 2):
        got.append(hop(s, got[-1], t2[2:5:2] if s == 1 else None))
    ends = [(n - 2, n - 1), (1, 0)]

    def last(c, after):
        return lax.ppermute(choose(sz, c, tie(here, after), *got[-1]), "row", ends)

    def leftovers(d, after):
        pairs = [(i, i ^ d) for i in range(n) if 0 < i ^ d < n - 1]
        return lax.ppermute(tie(lf, after), "row", pairs)

    spread = {1: leftovers(1, got[0])}
    first = last(0, (t2, spread[1]))
    need = longest(sz, here, own, got)
    need = lax.pmax(need, "col")
    second = last(1, need)
    spread.update({d: leftovers(d, need) for d in range(2, n)})
    spread = [spread[d] for d in range(1, n)]
    place, late, info = plan(sz, tie(here, need), own, got, first)
    told = lax.ppermute(tie(need, place), "row", ends)
    need = jnp.where(jnp.logical_or(me == 0, me == n - 1), told, need)[0]
    begun = main_part(sz, 1, info, place, t2, own, got, (first,))

    branch = sum((need > length).astype(jnp.int32) for length in sz.lengths[:-1])
    return lax.switch(
        branch,
        [functools.partial(last_hop, sz, length) for length in sz.lengths],
        info, place, late, t2, own, got, (first, second), lf, spread, begun,
    )


def solution(mesh):
    in_specs = (P("row", "col"), P("row", "col"), P("row", "col"), P("row", "col"))
    return jax.shard_map(
        functools.partial(body, mesh.shape["row"], mesh.shape["col"]),
        mesh=mesh,
        in_specs=in_specs,
        out_specs=P("row", "col"),
        check_vma=False,
    )
```

```python
import functools

import jax
import jax.numpy as jnp
from jax import lax
from jax.experimental import pallas as pl
from jax.experimental.pallas import tpu as pltpu
from jax.sharding import PartitionSpec as P

TILE = 128
PAIR = 2 * TILE
NOTE = 16
BF16 = jnp.bfloat16
LEFTS = 6
SMEM = pl.BlockSpec(memory_space=pltpu.SMEM)
VMEM = pl.BlockSpec(memory_space=pltpu.VMEM)
ANY = pl.BlockSpec(memory_space=pl.ANY)
HBM = pl.BlockSpec(memory_space=pltpu.HBM)
PARAMS = pltpu.CompilerParams(vmem_limit_bytes=40 << 20)
COST = pl.CostEstimate(flops=1 << 20, bytes_accessed=1 << 12, transcendentals=0)
LENGTHS = (8, 10, 12, 14, 16, 20)
FIRST = 28


def rows(tile, count=1):
    return pl.ds(pl.multiple_of(tile * TILE, TILE), count * TILE)


def tiles(count):
    return jax.ShapeDtypeStruct((count * TILE, TILE), BF16)


class Sizes:
    def __init__(self, n, k_tiles, n_tiles):
        self.n, self.kd, self.nd = n, k_tiles, n_tiles
        self.all = k_tiles * n_tiles
        self.main = self.all * 3 // 4
        self.first = self.main * FIRST // 48
        self.left = self.all - self.main
        self.stream = (n - 1) * self.left
        self.pairs = n_tiles // 2
        self.near = n // 2
        self.sure = (self.main // k_tiles) // 2
        lengths = {-(-f * self.stream // 48) for f in LENGTHS}
        self.lengths = sorted(lengths | {self.stream})

    def cut(self, c):
        start, stop = ((0, self.first), (self.first, self.main))[c]
        begin = NOTE + start * TILE if c else 0
        return start, stop - start, pl.ds(begin, NOTE + stop * TILE - begin)


def begin_kernel(
    sz, mask_v, v_mask_hbm, t2_mask_hbm, v, t2, main, lf, t2_out,
    v_v, t2_v, packed, v_mask, t2_mask, note, v_sem, sem,
):
    group = sz.nd // v_sem.shape[0]
    copies = []
    for g in range(v_sem.shape[0]):
        at = pl.ds(g * group * TILE, group * TILE)
        copies.append(pltpu.make_async_copy(v.at[:, at], v_v.at[:, at], v_sem.at[g]))
    mask_copy = pltpu.make_async_copy(v_mask_hbm, v_mask, sem.at[0])
    t2_copies = (
        pltpu.make_async_copy(t2_mask_hbm, t2_mask, sem.at[1]),
        pltpu.make_async_copy(t2, t2_v, sem.at[2]),
    )
    for copy in (mask_copy, *copies, *t2_copies):
        copy.start()
    note[...] = jnp.zeros_like(note)
    note[: sz.kd, : sz.nd] = (mask_v[...] > 0).astype(jnp.int32)
    mask_copy.wait()
    pos = jnp.int32(0)
    for c in range(sz.nd):
        if c % group == 0:
            copies[c // group].wait()
        for k in range(sz.kd):
            packed[rows(pos), :] = v_v[k * TILE : (k + 1) * TILE, c * TILE : (c + 1) * TILE]
            pos = pos + (v_mask[k, c] > 0).astype(jnp.int32)
    main[:NOTE, :] = note[...].astype(BF16)
    main[NOTE:, :] = packed[: sz.main * TILE, :]
    lf[...] = packed[sz.main * TILE :, :]
    for copy in t2_copies:
        copy.wait()
    for k in range(t2_mask.shape[0]):
        for i in range(t2_mask.shape[1]):
            at = (slice(i * TILE, (i + 1) * TILE), slice(k * TILE, (k + 1) * TILE))
            tile = t2_v[at]
            t2_out[at] = jnp.where(t2_mask[k, i] > 0, tile, jnp.zeros_like(tile))


def begin(sz, v, t2, v_mask, t2_mask):
    groups = 4 if sz.nd % 4 == 0 else 1
    return pl.pallas_call(
        functools.partial(begin_kernel, sz),
        out_shape=(
            jax.ShapeDtypeStruct((NOTE + sz.main * TILE, TILE), BF16),
            tiles(sz.left),
            jax.ShapeDtypeStruct(t2.shape, BF16),
        ),
        in_specs=[VMEM, HBM, HBM, HBM, HBM],
        out_specs=(VMEM, VMEM, VMEM),
        scratch_shapes=[
            pltpu.VMEM(v.shape, BF16),
            pltpu.VMEM(t2.shape, BF16),
            pltpu.VMEM((sz.all * TILE, TILE), BF16),
            pltpu.SMEM(v_mask.shape, jnp.int32),
            pltpu.SMEM(t2_mask.shape[::-1], jnp.int32),
            pltpu.VMEM((NOTE, TILE), jnp.int32),
            pltpu.SemaphoreType.DMA((groups,)),
            pltpu.SemaphoreType.DMA((3,)),
        ],
        compiler_params=pltpu.CompilerParams(vmem_limit_bytes=60 << 20),
        name="begin",
    )(v_mask, v_mask, t2_mask.T, v, t2)


def need_kernel(sz, here, *refs):
    n = sz.n
    parts, (out, notes, sem) = refs[: 2 * n - 3], refs[2 * n - 3 :]
    copies = [
        pltpu.make_async_copy(ref.at[pl.ds(0, NOTE), :], notes.at[i], sem.at[i])
        for i, ref in enumerate(parts)
    ]
    for copy in copies:
        copy.start()
    for copy in copies:
        copy.wait()
    me = here[0]
    sources = [me]
    for s in range(n - 2):
        sources += [me - 1 - s, me + 1 + s]
    to_up = to_down = jnp.int32(0)
    for i, z in enumerate(sources):
        count = jnp.sum(notes[i].astype(jnp.float32)).astype(jnp.int32)
        left = jnp.where(jnp.logical_and(z >= 0, z < n), jnp.maximum(count - sz.main, 0), 0)
        to_up = to_up + jnp.where(z == n - 1, 0, left)
        to_down = to_down + jnp.where(z == 0, 0, left)
    out[0] = jnp.maximum(to_up, to_down)


def longest(sz, here, own, got):
    ops = (own, *(part for hop in got for part in hop))
    return pl.pallas_call(
        functools.partial(need_kernel, sz),
        out_shape=jax.ShapeDtypeStruct((1,), jnp.int32),
        in_specs=[SMEM] + [ANY] * len(ops),
        out_specs=SMEM,
        scratch_shapes=[
            pltpu.VMEM((len(ops), NOTE, TILE), BF16),
            pltpu.SemaphoreType.DMA((len(ops),)),
        ],
        name="longest",
    )(here, *ops)


def from_source(sz, me, own, got, act, take=None):
    for m in range(sz.n):

        @pl.when(me == m)
        def _():
            for z in range(sz.n):
                if take is None or take(m, z):
                    act(z, own if z == m else got[abs(z - m) - 1][0 if z < m else 1])


def near_plan_kernel(sz, here, own, *refs):
    h = sz.near
    parts, (place, notes, wide, masks, note_sem, mask_sem) = refs[: 2 * h - 2], refs[2 * h - 2 :]

    def note_copy(z, ref):
        at = ref.at[pl.ds(0, NOTE), :]
        return pltpu.make_async_copy(at, notes.at[pl.ds(z % h * NOTE, NOTE), :], note_sem.at[z % h])

    got = [parts[2 * s : 2 * s + 2] for s in range(h - 1)]
    from_source(sz, here[0], own, got, lambda z, ref: note_copy(z, ref).start(), lambda m, z: m // h == z // h)
    for z in range(h):
        note_copy(z, own).wait()
    wide[...] = notes[...].astype(jnp.int32)
    mask_copy = pltpu.make_async_copy(wide, masks, mask_sem)
    mask_copy.start()
    mask_copy.wait()

    def column(c, counts):
        counts = list(counts)
        for z in range(h):
            for k in range(sz.kd):
                kept, p = masks[z * NOTE + k, c] > 0, counts[z]
                at = jnp.where(jnp.logical_and(kept, p < sz.main), z * sz.main + p, h * sz.main)
                place[(c * h + z) * sz.kd + k] = at
                counts[z] = p + kept.astype(jnp.int32)
        return tuple(counts)

    lax.fori_loop(0, 2 * sz.sure, column, (jnp.int32(0),) * h)


def near_plan(sz, here, own, got):
    h, ops = sz.near, (own, *(part for hop in got for part in hop))
    return pl.pallas_call(
        functools.partial(near_plan_kernel, sz),
        out_shape=jax.ShapeDtypeStruct((2 * sz.sure * h * sz.kd,), jnp.int32),
        in_specs=[SMEM] + [ANY] * len(ops),
        out_specs=SMEM,
        scratch_shapes=[
            pltpu.VMEM((h * NOTE, TILE), BF16),
            pltpu.VMEM((h * NOTE, TILE), jnp.int32),
            pltpu.SMEM((h * NOTE, TILE), jnp.int32),
            pltpu.SemaphoreType.DMA((h,)),
            pltpu.SemaphoreType.DMA,
        ],
        name="near_plan",
    )(here, *ops)


def plan_kernel(sz, here, *refs):
    n, me = sz.n, here[0]
    own, *parts, end = refs[: 2 * n - 2]
    place, late, info, notes, wide, masks, note_sem, mask_sem = refs[2 * n - 2 :]

    def note_copy(z, ref):
        at = ref.at[pl.ds(0, NOTE), :]
        return pltpu.make_async_copy(at, notes.at[pl.ds(z * NOTE, NOTE), :], note_sem.at[z])

    got = [parts[2 * s : 2 * s + 2] for s in range(n - 2)] + [(end, end)]
    from_source(sz, me, own, got, lambda z, ref: note_copy(z, ref).start())
    for z in range(n):
        note_copy(z, own).wait()
    wide[...] = notes[...].astype(jnp.int32)
    mask_copy = pltpu.make_async_copy(wide, masks, mask_sem)
    mask_copy.start()
    mask_copy.wait()

    def column(c, carry):
        counts, firsts, seconds = (list(carry[i * n : (i + 1) * n]) for i in range(3))
        for z in range(n):
            have = jnp.where(me == z, sz.all, sz.main)
            for k in range(sz.kd):
                i = c * n * sz.kd + z * sz.kd + k
                kept, p = masks[z * NOTE + k, c] > 0, counts[z]
                place[i] = jnp.where(jnp.logical_and(kept, p < have), z * sz.all + p, n * sz.all)
                late[i] = jnp.where(jnp.logical_and(kept, p >= have), p - sz.main, -1)
                counts[z] = p + kept.astype(jnp.int32)
            firsts[z] = jnp.minimum(firsts[z], jnp.where(counts[z] > sz.first, c, sz.nd))
            seconds[z] = jnp.minimum(seconds[z], jnp.where(counts[z] > have, c, sz.nd))
        return tuple(counts + firsts + seconds)

    start = (jnp.int32(0),) * n + (jnp.int32(sz.nd),) * (2 * n)
    out = lax.fori_loop(0, sz.nd, column, start)
    lefts = [jnp.maximum(c - sz.main, 0) for c in out[:n]]
    info[0] = me
    info[1] = jnp.int32(0)
    info[2] = functools.reduce(jnp.minimum, out[n : 2 * n], jnp.int32(2 * sz.sure)) // 2
    info[3] = functools.reduce(jnp.minimum, out[2 * n :], jnp.int32(sz.nd - 2)) // 2
    info[4] = jnp.int32(sz.pairs)
    info[5] = here[1]
    for z in range(n):
        info[LEFTS + z] = lefts[z]


def plan(sz, here, own, got, end):
    n, ops = sz.n, (own, *(part for hop in got for part in hop), end)
    return pl.pallas_call(
        functools.partial(plan_kernel, sz),
        out_shape=(
            jax.ShapeDtypeStruct((sz.n * sz.all,), jnp.int32),
            jax.ShapeDtypeStruct((sz.n * sz.all,), jnp.int32),
            jax.ShapeDtypeStruct((LEFTS + sz.n,), jnp.int32),
        ),
        in_specs=[SMEM] + [ANY] * len(ops),
        out_specs=(SMEM, SMEM, SMEM),
        scratch_shapes=[
            pltpu.VMEM((n * NOTE, TILE), BF16),
            pltpu.VMEM((n * NOTE, TILE), jnp.int32),
            pltpu.SMEM((n * NOTE, TILE), jnp.int32),
            pltpu.SemaphoreType.DMA((n,)),
            pltpu.SemaphoreType.DMA,
        ],
        name="plan",
    )(here, *ops)


def choose_kernel(sz, c, here, need, up, down, out, sem):
    at = sz.cut(c)[2]
    size = out.shape[0] - at.size
    if size:
        out[:size, :] = jnp.full((size, TILE), need[0].astype(jnp.float32)).astype(BF16)
    for mine, x in ((here[0] == sz.n - 2, up), (here[0] != sz.n - 2, down)):

        @pl.when(mine)
        def _():
            copy = pltpu.make_async_copy(x.at[at, :], out.at[pl.ds(size, at.size), :], sem)
            copy.start()
            copy.wait()


def choose(sz, c, here, need, up, down):
    return pl.pallas_call(
        functools.partial(choose_kernel, sz, c),
        out_shape=jax.ShapeDtypeStruct((sz.cut(c)[2].size + c * NOTE, TILE), BF16),
        in_specs=[SMEM, SMEM, ANY, ANY],
        out_specs=VMEM,
        scratch_shapes=[pltpu.SemaphoreType.DMA],
        compiler_params=PARAMS,
        name="choose",
    )(here, need, up, down)


def pool_kernel(sz, length, info, lf, *refs):
    n, me = sz.n, info[0]
    spread, (out, joined) = refs[: n - 1], refs[n - 1 :]
    for source, order in ((n - 2, range(n - 2, -1, -1)), (1, range(1, n))):

        @pl.when(me == source)
        def _():
            at = jnp.int32(0)
            for z in order:
                part = lf if z == source else spread[(z ^ source) - 1]
                joined[rows(at, sz.left), :] = part[...]
                at = at + info[LEFTS + z]
            out[...] = joined[: length * TILE, :]


def pool(sz, length, info, lf, spread):
    return pl.pallas_call(
        functools.partial(pool_kernel, sz, length),
        out_shape=tiles(length),
        in_specs=[SMEM] + [VMEM] * sz.n,
        out_specs=VMEM,
        scratch_shapes=[pltpu.VMEM((sz.stream * TILE, TILE), BF16)],
        compiler_params=PARAMS,
        name="pool",
    )(info, lf, *spread)


def out_copy(out, held, sem, slot, pair):
    if len(out.shape) == 3:
        return pltpu.make_async_copy(held.at[slot], out.at[pair], sem.at[slot])
    return pltpu.make_async_copy(
        held.at[slot], out.at[:, pl.ds(pl.multiple_of(pair * PAIR, PAIR), PAIR)], sem.at[slot]
    )


def t2_copies(act, col, part, t2, t2_v, sem, rs=(0, 1)):
    half, wide, nh = t2_v.shape[0] // 2, t2_v.shape[1] // len(t2), len(t2) // 2
    mine = col // nh == part
    for which, ds in ((mine, range(nh)), (jnp.logical_not(mine), range(nh, 2 * nh))):

        @pl.when(which)
        def _():
            for r in rs:
                at = pl.ds(pl.multiple_of(r * half, half), half)
                for d in ds:
                    to = t2_v.at[at, pl.ds(pl.multiple_of((col ^ d) * wide, wide), wide)]
                    act(pltpu.make_async_copy(t2[d].at[at, :], to, sem.at[d, r]))


def start(copy):
    copy.start()


def wait(copy):
    copy.wait()


def multiply(lo, hi, build, t2_wait, t2_v, out, held, sem, span=slice(None), acc=None, acc_v=None, acc_sem=None):
    half = held.shape[1] // 2

    def acc_copy(pair, slot):
        return pltpu.make_async_copy(acc.at[pair], acc_v.at[slot], acc_sem.at[slot])

    if acc is not None:

        @pl.when(lo < hi)
        def _():
            acc_copy(lo, 0).start()

    @pl.when(lo >= hi)
    def _():
        t2_wait((0, 1))

    @pl.loop(lo, hi)
    def _(pair):
        slot = lax.rem(pair - lo, 2)
        b = build(pair)
        if acc is not None:

            @pl.when(pair + 1 < hi)
            def _():
                acc_copy(pair + 1, 1 - slot).start()

            acc_copy(pair, slot).wait()

        @pl.when(pair >= lo + 2)
        def _():
            out_copy(out, held, sem, slot, pair).wait()

        @pl.loop(0, 2)
        def _(r):
            @pl.when(pair == lo)
            def _():
                t2_wait((r,))

            at = pl.ds(pl.multiple_of(r * half, half), half)
            product = jnp.dot(t2_v[at, span], b[...], preferred_element_type=jnp.float32)
            if acc is not None:
                product = product + acc_v[slot, at, :]
            held[slot, at, :] = product.astype(held.dtype)

        out_copy(out, held, sem, slot, pair).start()

    for back in (1, 2):

        @pl.when(hi - back >= lo)
        def _():
            out_copy(out, held, sem, lax.rem(hi - back - lo, 2), 0).wait()


def main_kernel(sz, chunks, n_t2, info, place, *refs):
    n = sz.n
    t2, refs = refs[:n_t2], refs[n_t2:]
    own, refs = refs[0], refs[1:]
    got, refs = [refs[2 * s : 2 * s + 2] for s in range(n - 2)], refs[2 * (n - 2) :]
    ends, refs = refs[:chunks], refs[chunks:]
    if chunks == 2:
        lf, acc, begun, out, rest, t2_v, packed, b, held, acc_v, in_sem, out_sem, acc_sem, t2_sem = refs
    else:
        acc, out, packed, b, held, acc_v, t2_v, in_sem, out_sem, acc_sem, t2_sem = refs
    me, col, h = info[0], info[5], sz.near
    far = jnp.where(me < h, h, 0)

    def chunk_copy(ref, z, c):
        start, count, at = sz.cut(c)
        size = count * TILE
        first = at.start + at.size - size if ref.shape[0] == NOTE + sz.main * TILE else ref.shape[0] - size
        to = packed.at[pl.ds((z * sz.all + start) * TILE, size), :]
        return pltpu.make_async_copy(ref.at[pl.ds(first, size), :], to, in_sem.at[z, c])

    def start_chunks(take):
        for c in range(chunks):
            parts = got + [(ends[c], ends[c])]
            from_source(sz, me, own, parts, lambda z, ref: chunk_copy(ref, z, c).start(), take)

    def wait_chunks(first):
        for i in range(h):
            for c in range(chunks):
                chunk_copy(own, first + i, c).wait()

    def t2_part(act, part, rs):
        t2_copies(act, col, part, t2, t2_v, t2_sem, rs)

    far_part = far // h
    start_chunks(lambda m, z: m // h != z // h)
    t2_part(start, far_part, (0, 1))
    if chunks == 2:
        start_chunks(lambda m, z: m // h == z // h)
        t2_part(start, 1 - far_part, (0, 1))
        left_copy = pltpu.make_async_copy(
            lf, packed.at[rows(me * sz.all + sz.main, sz.left), :], in_sem.at[0, 2]
        )
        left_copy.start()
    packed[n * sz.all * TILE :, :] = jnp.zeros((TILE, TILE), BF16)
    wait_chunks(far)

    def build(pair, to, first, count):
        @pl.loop(0, count * sz.kd)
        def _(k):
            for c in range(2):
                tile = packed[rows(place[((2 * pair + c) * n + first) * sz.kd + k]), :]
                to[rows(k), c * TILE : (c + 1) * TILE] = tile

        return to

    deep = h * sz.kd * TILE
    multiply(
        info[chunks], jnp.minimum(info[chunks + 1], sz.sure),
        lambda pair: build(pair, b.at[pl.ds(0, deep), :], far, h),
        lambda rs: t2_part(wait, far_part, rs), t2_v, out, held, out_sem,
        pl.ds(pl.multiple_of(far * sz.kd * TILE, deep), deep), acc, acc_v, acc_sem,
    )
    if chunks == 2:
        wait_chunks(h - far)
        left_copy.wait()
        t2_part(wait, 1 - far_part, (0, 1))
        multiply(
            jnp.int32(sz.sure), info[3], lambda pair: build(pair, b, 0, n),
            lambda rs: None, t2_v, out, held, out_sem,
        )
        for j in range(sz.pairs - sz.sure):
            build(sz.sure + j, rest.at[j], 0, n)


def early_kernel(sz, n_t2, here, place, *refs):
    h = sz.near
    t2, own, refs = refs[:n_t2], refs[n_t2], refs[n_t2 + 1 :]
    got, refs = [refs[2 * s : 2 * s + 2] for s in range(h - 1)], refs[2 * (h - 1) :]
    acc, packed, b, held, t2_v, in_sem, out_sem, t2_sem = refs
    me, col = here[0], here[1]

    def main_copy(ref, z):
        to = packed.at[pl.ds(z % h * sz.main * TILE, sz.main * TILE), :]
        return pltpu.make_async_copy(ref.at[pl.ds(NOTE, sz.main * TILE), :], to, in_sem.at[z % h])

    from_source(sz, me, own, got, lambda z, ref: main_copy(ref, z).start(), lambda m, z: m // h == z // h)
    part = me // h
    t2_copies(start, col, part, t2, t2_v, t2_sem)
    packed[h * sz.main * TILE :, :] = jnp.zeros((TILE, TILE), BF16)
    for z in range(h):
        main_copy(own, z).wait()

    def build(pair):
        @pl.loop(0, h * sz.kd)
        def _(k):
            for c in range(2):
                tile = packed[rows(place[(2 * pair + c) * h * sz.kd + k]), :]
                b[rows(k), c * TILE : (c + 1) * TILE] = tile

        return b

    deep = h * sz.kd * TILE
    span = pl.ds(pl.multiple_of(jnp.where(me < h, 0, deep), deep), deep)
    multiply(
        jnp.int32(0), jnp.int32(sz.sure), build,
        lambda rs: t2_copies(wait, col, part, t2, t2_v, t2_sem, rs), t2_v, acc, held, out_sem, span,
    )


def early_part(sz, here, place, t2, own, got):
    ij, cd = t2[0].shape[0], t2[0].shape[1] * len(t2)
    ops = [*t2, own, *(part for hop in got for part in hop)]
    return pl.pallas_call(
        functools.partial(early_kernel, sz, len(t2)),
        out_shape=pltpu.HBM((sz.sure, ij, PAIR), jnp.float32),
        in_specs=[SMEM, SMEM] + [ANY] * len(ops),
        out_specs=HBM,
        scratch_shapes=[
            pltpu.VMEM(((sz.near * sz.main + 1) * TILE, TILE), BF16),
            pltpu.VMEM((cd // 2, PAIR), BF16),
            pltpu.VMEM((2, ij, PAIR), jnp.float32),
            pltpu.VMEM((ij, cd), BF16),
            pltpu.SemaphoreType.DMA((sz.near,)),
            pltpu.SemaphoreType.DMA((2,)),
            pltpu.SemaphoreType.DMA((len(t2), 2)),
        ],
        compiler_params=PARAMS,
        cost_estimate=COST,
        name="early_part",
    )(here, place, *ops)


def main_part(sz, chunks, info, place, t2, own, got, ends, acc, lf=None, begun=None):
    ij, cd = t2[0].shape[0], t2[0].shape[1] * len(t2)
    ops = [*t2, own, *(part for hop in got for part in hop), *ends[:chunks]]
    out_shape = [pltpu.HBM((ij, sz.nd * TILE), BF16)]
    aliases = {}
    if chunks == 2:
        ops += [lf, acc, begun]
        aliases = {2 + len(ops) - 1: 0}
        out_shape.append(jax.ShapeDtypeStruct((sz.pairs - sz.sure, cd, PAIR), BF16))
        out_shape.append(pltpu.VMEM((ij, cd), BF16))
    else:
        ops += [acc]
    out = pl.pallas_call(
        functools.partial(main_kernel, sz, chunks, len(t2)),
        out_shape=out_shape,
        in_specs=[SMEM, SMEM] + [ANY] * len(ops),
        out_specs=[HBM, VMEM, VMEM][: 2 * chunks - 1],
        scratch_shapes=[
            pltpu.VMEM(((sz.n * sz.all + 1) * TILE, TILE), BF16),
            pltpu.VMEM((cd, PAIR), BF16),
            pltpu.VMEM((2, ij, PAIR), BF16),
            pltpu.VMEM((2, ij, PAIR), jnp.float32),
            *([pltpu.VMEM((ij, cd), BF16)] if chunks == 1 else []),
            pltpu.SemaphoreType.DMA((sz.n, 3)),
            pltpu.SemaphoreType.DMA((2,)),
            pltpu.SemaphoreType.DMA((2,)),
            pltpu.SemaphoreType.DMA((len(t2), 2)),
        ],
        input_output_aliases=aliases,
        compiler_params=PARAMS,
        cost_estimate=COST,
        name="main_part",
    )(info, place, *ops)
    return out if chunks == 2 else out[0]


def tail_kernel(sz, info, late, begun, rest, t2_v, top_end, low_end, *refs):
    n, me = sz.n, info[0]
    spread, (out, b, extra, held, in_sem, out_sem) = refs[: n - 1], refs[n - 1 :]
    is_end = jnp.logical_or(me == 0, me == n - 1)
    size = sz.left * TILE
    from_top, from_low = (
        [pltpu.make_async_copy(end, extra.at[pl.ds(0, end.shape[0]), :], in_sem.at[0])]
        for end in (top_end, low_end)
    )
    direct = [
        pltpu.make_async_copy(part, extra.at[pl.ds(i * size, size), :], in_sem.at[i])
        for i, part in enumerate(spread)
    ]

    def each(act):
        for which, copies in ((me == n - 1, from_top), (me == 0, from_low), (jnp.logical_not(is_end), direct)):

            @pl.when(which)
            def _():
                for copy in copies:
                    act(copy)

    each(lambda copy: copy.start())
    b[...] = rest[...]
    bases = []
    for z in range(n):
        top = sum((info[LEFTS + y] for y in range(z + 1, n - 1)), jnp.int32(0))
        bottom = sum((info[LEFTS + y] for y in range(1, z)), jnp.int32(0))
        base = jnp.where(is_end, jnp.where(me == 0, bottom, top), ((me ^ z) - 1) * sz.left)
        bases.append(base)

    each(lambda copy: copy.wait())
    for j in range(sz.pairs - sz.sure):
        for z in range(n):

            @pl.loop(0, sz.kd)
            def _(k):
                for c in range(2):
                    p = late[((2 * (sz.sure + j) + c) * n + z) * sz.kd + k]

                    @pl.when(p >= 0)
                    def _():
                        b[j, rows(z * sz.kd + k), c * TILE : (c + 1) * TILE] = extra[
                            rows(bases[z] + p), :
                        ]

    multiply(info[3], info[4], lambda pair: b.at[pair - sz.sure], lambda rs: None, t2_v, out, held, out_sem)


def tail_part(sz, info, late, t2_v, begun, rest, ends, spread):
    ij, cd = t2_v.shape
    pairs = sz.pairs - sz.sure
    region = max(ends[0].shape[0], (sz.n - 1) * sz.left * TILE)
    return pl.pallas_call(
        functools.partial(tail_kernel, sz),
        out_shape=pltpu.HBM(begun.shape, BF16),
        in_specs=[SMEM, SMEM, HBM, VMEM, VMEM] + [ANY] * (sz.n + 1),
        out_specs=HBM,
        scratch_shapes=[
            pltpu.VMEM((pairs, cd, PAIR), BF16),
            pltpu.VMEM((region, TILE), BF16),
            pltpu.VMEM((2, ij, PAIR), BF16),
            pltpu.SemaphoreType.DMA((sz.n - 1,)),
            pltpu.SemaphoreType.DMA((2,)),
        ],
        input_output_aliases={2: 0},
        compiler_params=PARAMS,
        cost_estimate=COST,
        name="tail_part",
    )(info, late, begun, rest, t2_v, *ends, *spread)


def last_hop(sz, length, info, place, late, t2, own, got, ends, acc, lf, spread, begun):
    n = sz.n
    joined = pool(sz, length, info, lf, spread)
    came = [lax.ppermute(joined, "row", pair) for pair in ([(n - 2, n - 1)], [(1, 0)])]
    begun, rest, t2_v = main_part(sz, 2, info, place, t2, own, got, ends, acc, lf, begun)
    return tail_part(sz, info, late, t2_v, begun, rest, came, spread)


def tie(value, after):
    return lax.optimization_barrier((value, after))[0]


def body(n, n_col, t2_amps, v_ints, t2_mask, v_mask):
    sz = Sizes(n, *v_mask.shape)
    me = lax.axis_index("row")
    here = jnp.stack([me, lax.axis_index("col")])
    own, lf, screened = begin(sz, v_ints, t2_amps, v_mask, t2_mask)

    def hop(s, value, after=None):
        up, down = value
        if after is not None:
            up, down = tie(up, after), tie(down, after)
        pairs = [(i, i + 1) for i in range(s, n - 1)]
        back = [(n - 1 - i, n - 1 - j) for i, j in pairs]
        return lax.ppermute(up, "row", pairs), lax.ppermute(down, "row", back)

    def across(value, d):
        return lax.ppermute(value, "col", [(i, i ^ d) for i in range(n_col)])

    t2 = {0: screened}
    got = [hop(0, (own, own))]
    for d in range(2, n_col, 2):
        t2[d] = across(screened if d < 6 else tie(screened, t2[2]), d)
    for d in range(0, n_col, 2):
        t2[d + 1] = across(t2[d], 1)
    t2 = [t2[d] for d in range(n_col)]
    for s in range(1, n - 2):
        got.append(hop(s, got[-1], t2[2:5:2] if s == 1 else None))
    ends = [(n - 2, n - 1), (1, 0)]

    def last(c, after):
        return lax.ppermute(choose(sz, c, here, after, *got[-1]), "row", ends)

    def leftovers(d, after):
        pairs = [(i, i ^ d) for i in range(n) if 0 < i ^ d < n - 1]
        return lax.ppermute(tie(lf, after), "row", pairs)

    spread = {1: leftovers(1, got[0])}
    near = got[: sz.near - 1]
    acc = early_part(sz, here, near_plan(sz, here, own, near), t2, own, near)
    first = last(0, tie(here, (t2, spread[1], acc)))
    need = longest(sz, here, own, got)
    need = lax.pmax(need, "col")
    second = last(1, need)
    spread.update({d: leftovers(d, need) for d in range(2, n)})
    spread = [spread[d] for d in range(1, n)]
    place, late, info = plan(sz, tie(here, need), own, got, first)
    begun = main_part(sz, 1, info, place, t2, own, got, (first,), acc)
    is_end = jnp.logical_or(me == 0, me == n - 1)
    need = jnp.where(is_end, tie(second, begun)[0, 0].astype(jnp.int32), need[0])

    branch = sum((need > length).astype(jnp.int32) for length in sz.lengths[:-1])
    return lax.switch(
        branch,
        [functools.partial(last_hop, sz, length) for length in sz.lengths],
        info, place, late, t2, own, got, (first, second), acc, lf, spread, begun,
    )


def solution(mesh):
    in_specs = (P("row", "col"), P("row", "col"), P("row", "col"), P("row", "col"))
    return jax.shard_map(
        functools.partial(body, mesh.shape["row"], mesh.shape["col"]),
        mesh=mesh,
        in_specs=in_specs,
        out_specs=P("row", "col"),
        check_vma=False,
    )
```

```python
import functools

import jax
import jax.numpy as jnp
from jax import lax
from jax.experimental import pallas as pl
from jax.experimental.pallas import tpu as pltpu
from jax.sharding import PartitionSpec as P

TILE = 128
PAIR = 2 * TILE
NOTE = 16
BF16 = jnp.bfloat16
LEFTS = 6
SMEM = pl.BlockSpec(memory_space=pltpu.SMEM)
VMEM = pl.BlockSpec(memory_space=pltpu.VMEM)
ANY = pl.BlockSpec(memory_space=pl.ANY)
HBM = pl.BlockSpec(memory_space=pltpu.HBM)
PARAMS = pltpu.CompilerParams(vmem_limit_bytes=40 << 20)
COST = pl.CostEstimate(flops=1 << 20, bytes_accessed=1 << 12, transcendentals=0)
LENGTHS = (8, 10, 12, 14, 16, 20)
FIRST = 24


def rows(tile, count=1):
    return pl.ds(pl.multiple_of(tile * TILE, TILE), count * TILE)


def tiles(count):
    return jax.ShapeDtypeStruct((count * TILE, TILE), BF16)


class Sizes:
    def __init__(self, n, k_tiles, n_tiles):
        self.n, self.kd, self.nd = n, k_tiles, n_tiles
        self.all = k_tiles * n_tiles
        self.main = self.all * 3 // 4
        self.first = self.main * FIRST // 48
        self.left = self.all - self.main
        self.stream = (n - 1) * self.left
        self.pairs = n_tiles // 2
        self.near = n // 2
        self.sure = (self.main // k_tiles) // 2
        lengths = {-(-f * self.stream // 48) for f in LENGTHS}
        self.lengths = sorted(lengths | {self.stream})

    def cut(self, c):
        start, stop = ((0, self.first), (self.first, self.main))[c]
        begin = NOTE + start * TILE if c else 0
        return start, stop - start, pl.ds(begin, NOTE + stop * TILE - begin)


def begin_kernel(
    sz, mask_v, v_mask_hbm, t2_mask_hbm, v, t2, main, lf, t2_out,
    v_v, t2_v, packed, v_mask, t2_mask, note, v_sem, sem,
):
    group = sz.nd // v_sem.shape[0]
    copies = []
    for g in range(v_sem.shape[0]):
        at = pl.ds(g * group * TILE, group * TILE)
        copies.append(pltpu.make_async_copy(v.at[:, at], v_v.at[:, at], v_sem.at[g]))
    mask_copy = pltpu.make_async_copy(v_mask_hbm, v_mask, sem.at[0])
    t2_copies = (
        pltpu.make_async_copy(t2_mask_hbm, t2_mask, sem.at[1]),
        pltpu.make_async_copy(t2, t2_v, sem.at[2]),
    )
    for copy in (mask_copy, *copies, *t2_copies):
        copy.start()
    note[...] = jnp.zeros_like(note)
    note[: sz.kd, : sz.nd] = (mask_v[...] > 0).astype(jnp.int32)
    mask_copy.wait()
    pos = jnp.int32(0)
    for c in range(sz.nd):
        if c % group == 0:
            copies[c // group].wait()
        for k in range(sz.kd):
            packed[rows(pos), :] = v_v[k * TILE : (k + 1) * TILE, c * TILE : (c + 1) * TILE]
            pos = pos + (v_mask[k, c] > 0).astype(jnp.int32)
    main[:NOTE, :] = note[...].astype(BF16)
    main[NOTE:, :] = packed[: sz.main * TILE, :]
    lf[...] = packed[sz.main * TILE :, :]
    for copy in t2_copies:
        copy.wait()
    for k in range(t2_mask.shape[0]):
        for i in range(t2_mask.shape[1]):
            at = (slice(i * TILE, (i + 1) * TILE), slice(k * TILE, (k + 1) * TILE))
            tile = t2_v[at]
            t2_out[at] = jnp.where(t2_mask[k, i] > 0, tile, jnp.zeros_like(tile))


def begin(sz, v, t2, v_mask, t2_mask):
    groups = 4 if sz.nd % 4 == 0 else 1
    return pl.pallas_call(
        functools.partial(begin_kernel, sz),
        out_shape=(
            jax.ShapeDtypeStruct((NOTE + sz.main * TILE, TILE), BF16),
            tiles(sz.left),
            jax.ShapeDtypeStruct(t2.shape, BF16),
        ),
        in_specs=[VMEM, HBM, HBM, HBM, HBM],
        out_specs=(VMEM, VMEM, VMEM),
        scratch_shapes=[
            pltpu.VMEM(v.shape, BF16),
            pltpu.VMEM(t2.shape, BF16),
            pltpu.VMEM((sz.all * TILE, TILE), BF16),
            pltpu.SMEM(v_mask.shape, jnp.int32),
            pltpu.SMEM(t2_mask.shape[::-1], jnp.int32),
            pltpu.VMEM((NOTE, TILE), jnp.int32),
            pltpu.SemaphoreType.DMA((groups,)),
            pltpu.SemaphoreType.DMA((3,)),
        ],
        compiler_params=pltpu.CompilerParams(vmem_limit_bytes=60 << 20),
        name="begin",
    )(v_mask, v_mask, t2_mask.T, v, t2)


def need_kernel(sz, here, *refs):
    n = sz.n
    parts, (out, notes, sem) = refs[: 2 * n - 3], refs[2 * n - 3 :]
    copies = [
        pltpu.make_async_copy(ref.at[pl.ds(0, NOTE), :], notes.at[i], sem.at[i])
        for i, ref in enumerate(parts)
    ]
    for copy in copies:
        copy.start()
    for copy in copies:
        copy.wait()
    me = here[0]
    sources = [me]
    for s in range(n - 2):
        sources += [me - 1 - s, me + 1 + s]
    to_up = to_down = jnp.int32(0)
    for i, z in enumerate(sources):
        count = jnp.sum(notes[i].astype(jnp.float32)).astype(jnp.int32)
        left = jnp.where(jnp.logical_and(z >= 0, z < n), jnp.maximum(count - sz.main, 0), 0)
        to_up = to_up + jnp.where(z == n - 1, 0, left)
        to_down = to_down + jnp.where(z == 0, 0, left)
    out[0] = jnp.maximum(to_up, to_down)


def from_source(sz, me, own, got, act, take=None):
    for m in range(sz.n):

        @pl.when(me == m)
        def _():
            for z in range(sz.n):
                if take is None or take(m, z):
                    act(z, own if z == m else got[abs(z - m) - 1][0 if z < m else 1])


def near_plan_kernel(sz, here, own, *refs):
    h = sz.near
    parts, (place, notes, wide, masks, note_sem, mask_sem) = refs[: 2 * h - 2], refs[2 * h - 2 :]

    def note_copy(z, ref):
        at = ref.at[pl.ds(0, NOTE), :]
        return pltpu.make_async_copy(at, notes.at[pl.ds(z % h * NOTE, NOTE), :], note_sem.at[z % h])

    got = [parts[2 * s : 2 * s + 2] for s in range(h - 1)]
    from_source(sz, here[0], own, got, lambda z, ref: note_copy(z, ref).start(), lambda m, z: m // h == z // h)
    for z in range(h):
        note_copy(z, own).wait()
    wide[...] = notes[...].astype(jnp.int32)
    mask_copy = pltpu.make_async_copy(wide, masks, mask_sem)
    mask_copy.start()
    mask_copy.wait()

    def column(c, counts):
        counts = list(counts)
        keeps = [[masks[z * NOTE + k, c] > 0 for k in range(sz.kd)] for z in range(h)]
        for z in range(h):
            for k in range(sz.kd):
                kept, p = keeps[z][k], counts[z]
                at = jnp.where(jnp.logical_and(kept, p < sz.main), z * sz.main + p, h * sz.main)
                place[(c * h + z) * sz.kd + k] = at
                counts[z] = p + kept.astype(jnp.int32)
        return tuple(counts)

    lax.fori_loop(0, 2 * sz.sure, column, (jnp.int32(0),) * h)


def near_plan(sz, here, own, got):
    h, ops = sz.near, (own, *(part for hop in got for part in hop))
    return pl.pallas_call(
        functools.partial(near_plan_kernel, sz),
        out_shape=jax.ShapeDtypeStruct((2 * sz.sure * h * sz.kd,), jnp.int32),
        in_specs=[SMEM] + [ANY] * len(ops),
        out_specs=SMEM,
        scratch_shapes=[
            pltpu.VMEM((h * NOTE, TILE), BF16),
            pltpu.VMEM((h * NOTE, TILE), jnp.int32),
            pltpu.SMEM((h * NOTE, TILE), jnp.int32),
            pltpu.SemaphoreType.DMA((h,)),
            pltpu.SemaphoreType.DMA,
        ],
        name="near_plan",
    )(here, *ops)


def plan_kernel(sz, here, *refs):
    n, me = sz.n, here[0]
    own, *parts, end = refs[: 2 * n - 2]
    place, late, info, notes, wide, masks, note_sem, mask_sem = refs[2 * n - 2 :]

    def note_copy(z, ref):
        at = ref.at[pl.ds(0, NOTE), :]
        return pltpu.make_async_copy(at, notes.at[pl.ds(z * NOTE, NOTE), :], note_sem.at[z])

    got = [parts[2 * s : 2 * s + 2] for s in range(n - 2)] + [(end, end)]
    from_source(sz, me, own, got, lambda z, ref: note_copy(z, ref).start())
    for z in range(n):
        note_copy(z, own).wait()
    wide[...] = notes[...].astype(jnp.int32)
    mask_copy = pltpu.make_async_copy(wide, masks, mask_sem)
    mask_copy.start()
    mask_copy.wait()

    def column(c, carry):
        counts, firsts, seconds = (list(carry[i * n : (i + 1) * n]) for i in range(3))
        keeps = [[masks[z * NOTE + k, c] > 0 for k in range(sz.kd)] for z in range(n)]
        for z in range(n):
            have = jnp.where(me == z, sz.all, sz.main)
            for k in range(sz.kd):
                i = c * n * sz.kd + z * sz.kd + k
                kept, p = keeps[z][k], counts[z]
                place[i] = jnp.where(jnp.logical_and(kept, p < have), z * sz.all + p, n * sz.all)
                late[i] = jnp.where(jnp.logical_and(kept, p >= have), p - sz.main, -1)
                counts[z] = p + kept.astype(jnp.int32)
            firsts[z] = jnp.minimum(firsts[z], jnp.where(counts[z] > sz.first, c, sz.nd))
            seconds[z] = jnp.minimum(seconds[z], jnp.where(counts[z] > have, c, sz.nd))
        return tuple(counts + firsts + seconds)

    start = (jnp.int32(0),) * n + (jnp.int32(sz.nd),) * (2 * n)
    out = lax.fori_loop(0, sz.nd, column, start)
    lefts = [jnp.maximum(c - sz.main, 0) for c in out[:n]]
    info[0] = me
    info[1] = jnp.int32(0)
    info[2] = functools.reduce(jnp.minimum, out[n : 2 * n], jnp.int32(2 * sz.sure)) // 2
    info[3] = functools.reduce(jnp.minimum, out[2 * n :], jnp.int32(sz.nd - 2)) // 2
    info[4] = jnp.int32(sz.pairs)
    info[5] = here[1]
    for z in range(n):
        info[LEFTS + z] = lefts[z]


def plan(sz, here, own, got, end):
    n, ops = sz.n, (own, *(part for hop in got for part in hop), end)
    return pl.pallas_call(
        functools.partial(plan_kernel, sz),
        out_shape=(
            jax.ShapeDtypeStruct((sz.n * sz.all,), jnp.int32),
            jax.ShapeDtypeStruct((sz.n * sz.all,), jnp.int32),
            jax.ShapeDtypeStruct((LEFTS + sz.n,), jnp.int32),
        ),
        in_specs=[SMEM] + [ANY] * len(ops),
        out_specs=(SMEM, SMEM, SMEM),
        scratch_shapes=[
            pltpu.VMEM((n * NOTE, TILE), BF16),
            pltpu.VMEM((n * NOTE, TILE), jnp.int32),
            pltpu.SMEM((n * NOTE, TILE), jnp.int32),
            pltpu.SemaphoreType.DMA((n,)),
            pltpu.SemaphoreType.DMA,
        ],
        name="plan",
    )(here, *ops)


def choose_kernel(sz, c, here, need, up, down, out, sem):
    at = sz.cut(c)[2]
    size = out.shape[0] - at.size
    if size:
        out[:size, :] = jnp.full((size, TILE), need[0].astype(jnp.float32)).astype(BF16)
    for mine, x in ((here[0] == sz.n - 2, up), (here[0] != sz.n - 2, down)):

        @pl.when(mine)
        def _():
            copy = pltpu.make_async_copy(x.at[at, :], out.at[pl.ds(size, at.size), :], sem)
            copy.start()
            copy.wait()


def choose(sz, c, here, need, up, down):
    return pl.pallas_call(
        functools.partial(choose_kernel, sz, c),
        out_shape=jax.ShapeDtypeStruct((sz.cut(c)[2].size + c * NOTE, TILE), BF16),
        in_specs=[SMEM, SMEM, ANY, ANY],
        out_specs=VMEM,
        scratch_shapes=[pltpu.SemaphoreType.DMA],
        compiler_params=PARAMS,
        name="choose",
    )(here, need, up, down)


def first_kernel(sz, here, *refs):
    parts, (out, need, notes, note_sem, sem) = refs[: 2 * sz.n - 3], refs[2 * sz.n - 3 :]
    at = sz.cut(0)[2]
    up, down = (pltpu.make_async_copy(x.at[at, :], out, sem) for x in parts[-2:])
    mine = here[0] == sz.n - 2
    pl.when(mine)(lambda: up.start())
    pl.when(jnp.logical_not(mine))(lambda: down.start())
    need_kernel(sz, here, *parts, need, notes, note_sem)
    up.wait()


def choose_first(sz, here, own, got):
    ops = (own, *(part for hop in got for part in hop))
    return pl.pallas_call(
        functools.partial(first_kernel, sz),
        out_shape=(
            jax.ShapeDtypeStruct((sz.cut(0)[2].size, TILE), BF16),
            jax.ShapeDtypeStruct((1,), jnp.int32),
        ),
        in_specs=[SMEM] + [ANY] * len(ops),
        out_specs=(VMEM, SMEM),
        scratch_shapes=[
            pltpu.VMEM((len(ops), NOTE, TILE), BF16),
            pltpu.SemaphoreType.DMA((len(ops),)),
            pltpu.SemaphoreType.DMA,
        ],
        compiler_params=PARAMS,
        name="choose_first",
    )(here, *ops)


def pool_kernel(sz, length, info, lf, *refs):
    n, me = sz.n, info[0]
    spread, (out, joined) = refs[: n - 1], refs[n - 1 :]
    for source, order in ((n - 2, range(n - 2, -1, -1)), (1, range(1, n))):

        @pl.when(me == source)
        def _():
            at = jnp.int32(0)
            for z in order:
                part = lf if z == source else spread[(z ^ source) - 1]
                joined[rows(at, sz.left), :] = part[...]
                at = at + info[LEFTS + z]
            out[...] = joined[: length * TILE, :]


def pool(sz, length, info, lf, spread):
    return pl.pallas_call(
        functools.partial(pool_kernel, sz, length),
        out_shape=tiles(length),
        in_specs=[SMEM] + [VMEM] * sz.n,
        out_specs=VMEM,
        scratch_shapes=[pltpu.VMEM((sz.stream * TILE, TILE), BF16)],
        compiler_params=PARAMS,
        name="pool",
    )(info, lf, *spread)


def out_copy(out, held, sem, slot, pair):
    if len(out.shape) == 3:
        return pltpu.make_async_copy(held.at[slot], out.at[pair], sem.at[slot])
    return pltpu.make_async_copy(
        held.at[slot], out.at[:, pl.ds(pl.multiple_of(pair * PAIR, PAIR), PAIR)], sem.at[slot]
    )


def t2_copies(act, col, part, t2, t2_v, sem, rs=(0, 1)):
    half, wide, nh = t2_v.shape[0] // 2, t2_v.shape[1] // len(t2), len(t2) // 2
    mine = col // nh == part
    for which, ds in ((mine, range(nh)), (jnp.logical_not(mine), range(nh, 2 * nh))):

        @pl.when(which)
        def _():
            for r in rs:
                at = pl.ds(pl.multiple_of(r * half, half), half)
                for d in ds:
                    to = t2_v.at[at, pl.ds(pl.multiple_of((col ^ d) * wide, wide), wide)]
                    act(pltpu.make_async_copy(t2[d].at[at, :], to, sem.at[d, r]))


def start(copy):
    copy.start()


def wait(copy):
    copy.wait()


def multiply(lo, hi, build, t2_wait, t2_v, out, held, sem, span=slice(None), acc=None, acc_v=None, acc_sem=None):
    half = held.shape[1] // 2

    def acc_copy(pair, slot):
        return pltpu.make_async_copy(acc.at[pair], acc_v.at[slot], acc_sem.at[slot])

    if acc is not None:

        @pl.when(lo < hi)
        def _():
            acc_copy(lo, 0).start()

    @pl.when(lo >= hi)
    def _():
        t2_wait((0, 1))

    @pl.loop(lo, hi)
    def _(pair):
        slot = lax.rem(pair - lo, 2)
        b = build(pair)
        if acc is not None:

            @pl.when(pair + 1 < hi)
            def _():
                acc_copy(pair + 1, 1 - slot).start()

            acc_copy(pair, slot).wait()

        @pl.when(pair >= lo + 2)
        def _():
            out_copy(out, held, sem, slot, pair).wait()

        @pl.loop(0, 2)
        def _(r):
            @pl.when(pair == lo)
            def _():
                t2_wait((r,))

            at = pl.ds(pl.multiple_of(r * half, half), half)
            product = jnp.dot(t2_v[at, span], b[...], preferred_element_type=jnp.float32)
            if acc is not None:
                product = product + acc_v[slot, at, :]
            held[slot, at, :] = product.astype(held.dtype)

        out_copy(out, held, sem, slot, pair).start()

    for back in (1, 2):

        @pl.when(hi - back >= lo)
        def _():
            out_copy(out, held, sem, lax.rem(hi - back - lo, 2), 0).wait()


def main_kernel(sz, chunks, n_t2, info, place, *refs):
    n = sz.n
    t2, refs = refs[:n_t2], refs[n_t2:]
    own, refs = refs[0], refs[1:]
    got, refs = [refs[2 * s : 2 * s + 2] for s in range(n - 2)], refs[2 * (n - 2) :]
    ends, refs = refs[:chunks], refs[chunks:]
    if chunks == 2:
        lf, acc, begun, out, rest, t2_v, packed, b, held, acc_v, in_sem, out_sem, acc_sem, t2_sem = refs
    else:
        acc, out, packed, b, held, acc_v, t2_v, in_sem, out_sem, acc_sem, t2_sem = refs
    me, col, h = info[0], info[5], sz.near
    far = jnp.where(me < h, h, 0)

    def chunk_copy(ref, z, c):
        start, count, at = sz.cut(c)
        size = count * TILE
        first = at.start + at.size - size if ref.shape[0] == NOTE + sz.main * TILE else ref.shape[0] - size
        to = packed.at[pl.ds((z * sz.all + start) * TILE, size), :]
        return pltpu.make_async_copy(ref.at[pl.ds(first, size), :], to, in_sem.at[z, c])

    def start_chunks(take):
        for c in range(chunks):
            parts = got + [(ends[c], ends[c])]
            from_source(sz, me, own, parts, lambda z, ref: chunk_copy(ref, z, c).start(), take)

    def wait_chunks(first):
        for i in range(h):
            for c in range(chunks):
                chunk_copy(own, first + i, c).wait()

    def t2_part(act, part, rs):
        t2_copies(act, col, part, t2, t2_v, t2_sem, rs)

    far_part = far // h
    start_chunks(lambda m, z: m // h != z // h)
    t2_part(start, far_part, (0, 1))
    if chunks == 2:
        start_chunks(lambda m, z: m // h == z // h)
        t2_part(start, 1 - far_part, (0, 1))
        left_copy = pltpu.make_async_copy(
            lf, packed.at[rows(me * sz.all + sz.main, sz.left), :], in_sem.at[0, 2]
        )
        left_copy.start()
    packed[n * sz.all * TILE :, :] = jnp.zeros((TILE, TILE), BF16)
    wait_chunks(far)

    def build(pair, to, first, count):
        @pl.loop(0, count * sz.kd)
        def _(k):
            for c in range(2):
                tile = packed[rows(place[((2 * pair + c) * n + first) * sz.kd + k]), :]
                to[rows(k), c * TILE : (c + 1) * TILE] = tile

        return to

    deep = h * sz.kd * TILE
    multiply(
        info[chunks], jnp.minimum(info[chunks + 1], sz.sure),
        lambda pair: build(pair, b.at[pl.ds(0, deep), :], far, h),
        lambda rs: t2_part(wait, far_part, rs), t2_v, out, held, out_sem,
        pl.ds(pl.multiple_of(far * sz.kd * TILE, deep), deep), acc, acc_v, acc_sem,
    )
    if chunks == 2:
        wait_chunks(h - far)
        left_copy.wait()
        t2_part(wait, 1 - far_part, (0, 1))
        multiply(
            jnp.int32(sz.sure), info[3], lambda pair: build(pair, b, 0, n),
            lambda rs: None, t2_v, out, held, out_sem,
        )
        for j in range(sz.pairs - sz.sure):

            @pl.when(sz.sure + j >= info[3])
            def _():
                build(sz.sure + j, rest.at[j], 0, n)


def early_kernel(sz, n_t2, here, place, *refs):
    h = sz.near
    t2, own, refs = refs[:n_t2], refs[n_t2], refs[n_t2 + 1 :]
    got, refs = [refs[2 * s : 2 * s + 2] for s in range(h - 1)], refs[2 * (h - 1) :]
    acc, packed, b, held, t2_v, in_sem, out_sem, t2_sem = refs
    me, col = here[0], here[1]

    def main_copy(ref, z):
        to = packed.at[pl.ds(z % h * sz.main * TILE, sz.main * TILE), :]
        return pltpu.make_async_copy(ref.at[pl.ds(NOTE, sz.main * TILE), :], to, in_sem.at[z % h])

    from_source(sz, me, own, got, lambda z, ref: main_copy(ref, z).start(), lambda m, z: m // h == z // h)
    part = me // h
    t2_copies(start, col, part, t2, t2_v, t2_sem)
    packed[h * sz.main * TILE :, :] = jnp.zeros((TILE, TILE), BF16)
    for z in range(h):
        main_copy(own, z).wait()

    def build(pair):
        @pl.loop(0, h * sz.kd)
        def _(k):
            for c in range(2):
                tile = packed[rows(place[(2 * pair + c) * h * sz.kd + k]), :]
                b[rows(k), c * TILE : (c + 1) * TILE] = tile

        return b

    deep = h * sz.kd * TILE
    span = pl.ds(pl.multiple_of(jnp.where(me < h, 0, deep), deep), deep)
    multiply(
        jnp.int32(0), jnp.int32(sz.sure), build,
        lambda rs: t2_copies(wait, col, part, t2, t2_v, t2_sem, rs), t2_v, acc, held, out_sem, span,
    )


def early_part(sz, here, place, t2, own, got):
    ij, cd = t2[0].shape[0], t2[0].shape[1] * len(t2)
    ops = [*t2, own, *(part for hop in got for part in hop)]
    return pl.pallas_call(
        functools.partial(early_kernel, sz, len(t2)),
        out_shape=pltpu.HBM((sz.sure, ij, PAIR), jnp.float32),
        in_specs=[SMEM, SMEM] + [ANY] * len(ops),
        out_specs=HBM,
        scratch_shapes=[
            pltpu.VMEM(((sz.near * sz.main + 1) * TILE, TILE), BF16),
            pltpu.VMEM((cd // 2, PAIR), BF16),
            pltpu.VMEM((2, ij, PAIR), jnp.float32),
            pltpu.VMEM((ij, cd), BF16),
            pltpu.SemaphoreType.DMA((sz.near,)),
            pltpu.SemaphoreType.DMA((2,)),
            pltpu.SemaphoreType.DMA((len(t2), 2)),
        ],
        compiler_params=PARAMS,
        cost_estimate=COST,
        name="early_part",
    )(here, place, *ops)


def main_part(sz, chunks, info, place, t2, own, got, ends, acc, lf=None, begun=None):
    ij, cd = t2[0].shape[0], t2[0].shape[1] * len(t2)
    ops = [*t2, own, *(part for hop in got for part in hop), *ends[:chunks]]
    out_shape = [pltpu.HBM((ij, sz.nd * TILE), BF16)]
    aliases = {}
    if chunks == 2:
        ops += [lf, acc, begun]
        aliases = {2 + len(ops) - 1: 0}
        out_shape.append(jax.ShapeDtypeStruct((sz.pairs - sz.sure, cd, PAIR), BF16))
        out_shape.append(pltpu.VMEM((ij, cd), BF16))
    else:
        ops += [acc]
    out = pl.pallas_call(
        functools.partial(main_kernel, sz, chunks, len(t2)),
        out_shape=out_shape,
        in_specs=[SMEM, SMEM] + [ANY] * len(ops),
        out_specs=[HBM, VMEM, VMEM][: 2 * chunks - 1],
        scratch_shapes=[
            pltpu.VMEM(((sz.n * sz.all + 1) * TILE, TILE), BF16),
            pltpu.VMEM((cd, PAIR), BF16),
            pltpu.VMEM((2, ij, PAIR), BF16),
            pltpu.VMEM((2, ij, PAIR), jnp.float32),
            *([pltpu.VMEM((ij, cd), BF16)] if chunks == 1 else []),
            pltpu.SemaphoreType.DMA((sz.n, 3)),
            pltpu.SemaphoreType.DMA((2,)),
            pltpu.SemaphoreType.DMA((2,)),
            pltpu.SemaphoreType.DMA((len(t2), 2)),
        ],
        input_output_aliases=aliases,
        compiler_params=PARAMS,
        cost_estimate=COST,
        name="main_part",
    )(info, place, *ops)
    return out if chunks == 2 else out[0]


def tail_kernel(sz, info, late, begun, rest, t2_v, end, *refs):
    n, me, whole = sz.n, info[0], info[3]
    spread, (out, b, extra, held, in_sem, out_sem) = refs[: n - 1], refs[n - 1 :]
    is_end = jnp.logical_or(me == 0, me == n - 1)
    size = sz.left * TILE
    from_pool = [pltpu.make_async_copy(end, extra.at[pl.ds(0, end.shape[0]), :], in_sem.at[0])]
    direct = [
        pltpu.make_async_copy(part, extra.at[pl.ds(i * size, size), :], in_sem.at[i])
        for i, part in enumerate(spread)
    ]

    def each(act):
        for which, copies in ((is_end, from_pool), (jnp.logical_not(is_end), direct)):

            @pl.when(which)
            def _():
                for copy in copies:
                    act(copy)

    each(lambda copy: copy.start())
    for j in range(sz.pairs - sz.sure):

        @pl.when(sz.sure + j >= whole)
        def _():
            b[j] = rest[j]

    bases = []
    for z in range(n):
        top = sum((info[LEFTS + y] for y in range(z + 1, n - 1)), jnp.int32(0))
        bottom = sum((info[LEFTS + y] for y in range(1, z)), jnp.int32(0))
        base = jnp.where(is_end, jnp.where(me == 0, bottom, top), ((me ^ z) - 1) * sz.left)
        bases.append(base)

    each(lambda copy: copy.wait())
    for j in range(sz.pairs - sz.sure):

        @pl.when(sz.sure + j >= whole)
        def _():
            for z in range(n):

                @pl.loop(0, sz.kd)
                def _(k):
                    for c in range(2):
                        p = late[((2 * (sz.sure + j) + c) * n + z) * sz.kd + k]

                        @pl.when(p >= 0)
                        def _():
                            b[j, rows(z * sz.kd + k), c * TILE : (c + 1) * TILE] = extra[
                                rows(bases[z] + p), :
                            ]

    multiply(whole, info[4], lambda pair: b.at[pair - sz.sure], lambda rs: None, t2_v, out, held, out_sem)


def tail_part(sz, info, late, t2_v, begun, rest, end, spread):
    ij, cd = t2_v.shape
    pairs = sz.pairs - sz.sure
    region = max(end.shape[0], (sz.n - 1) * sz.left * TILE)
    return pl.pallas_call(
        functools.partial(tail_kernel, sz),
        out_shape=pltpu.HBM(begun.shape, BF16),
        in_specs=[SMEM, SMEM, HBM, VMEM, VMEM] + [ANY] * sz.n,
        out_specs=HBM,
        scratch_shapes=[
            pltpu.VMEM((pairs, cd, PAIR), BF16),
            pltpu.VMEM((region, TILE), BF16),
            pltpu.VMEM((2, ij, PAIR), BF16),
            pltpu.SemaphoreType.DMA((sz.n - 1,)),
            pltpu.SemaphoreType.DMA((2,)),
        ],
        input_output_aliases={2: 0},
        compiler_params=PARAMS,
        cost_estimate=COST,
        name="tail_part",
    )(info, late, begun, rest, t2_v, end, *spread)


def last_hop(sz, length, info, place, late, t2, own, got, ends, acc, lf, spread, begun):
    n = sz.n
    came = lax.ppermute(pool(sz, length, info, lf, spread), "row", [(n - 2, n - 1), (1, 0)])
    begun, rest, t2_v = main_part(sz, 2, info, place, t2, own, got, ends, acc, lf, begun)
    return tail_part(sz, info, late, t2_v, begun, rest, came, spread)


def tie(value, after):
    return lax.optimization_barrier((value, after))[0]


def body(n, n_col, t2_amps, v_ints, t2_mask, v_mask):
    sz = Sizes(n, *v_mask.shape)
    me = lax.axis_index("row")
    here = jnp.stack([me, lax.axis_index("col")])
    own, lf, screened = begin(sz, v_ints, t2_amps, v_mask, t2_mask)

    def hop(s, value, after=None):
        up, down = value
        if after is not None:
            up, down = tie(up, after), tie(down, after)
        pairs = [(i, i + 1) for i in range(s, n - 1)]
        back = [(n - 1 - i, n - 1 - j) for i, j in pairs]
        return lax.ppermute(up, "row", pairs), lax.ppermute(down, "row", back)

    def across(value, d):
        return lax.ppermute(value, "col", [(i, i ^ d) for i in range(n_col)])

    t2 = {0: screened}
    got = [hop(0, (own, own))]
    for d in range(2, n_col, 2):
        t2[d] = across(screened if d < 6 else tie(screened, t2[2]), d)
    for s in range(1, n - 2):
        got.append(hop(s, got[-1], (t2[2], t2[4]) if s == 1 else None))
    near = got[: sz.near - 1]
    near_place = near_plan(sz, here, own, near)
    for d in range(0, n_col, 2):
        t2[d + 1] = across(tie(t2[d], near_place) if d == 4 else t2[d], 1)
    t2 = [t2[d] for d in range(n_col)]
    ends = [(n - 2, n - 1), (1, 0)]

    def leftovers(d, after):
        pairs = [(i, i ^ d) for i in range(n) if 0 < i ^ d < n - 1]
        return lax.ppermute(tie(lf, after), "row", pairs)

    spread = {1: leftovers(1, got[0])}
    acc = early_part(sz, here, near_place, t2, own, near)
    first, need = choose_first(sz, tie(here, (t2, spread[1], acc)), own, got)
    first = lax.ppermute(first, "row", ends)
    need = lax.pmax(need, "col")
    second = lax.ppermute(choose(sz, 1, here, need, *got[-1]), "row", ends)
    spread.update({d: leftovers(d, need) for d in range(2, n)})
    spread = [spread[d] for d in range(1, n)]
    place, late, info = plan(sz, tie(here, need), own, got, first)
    begun = main_part(sz, 1, info, place, t2, own, got, (first,), acc)
    is_end = jnp.logical_or(me == 0, me == n - 1)
    need = jnp.where(is_end, tie(second, begun)[0, 0].astype(jnp.int32), need[0])

    branch = sum((need > length).astype(jnp.int32) for length in sz.lengths[:-1])
    return lax.switch(
        branch,
        [functools.partial(last_hop, sz, length) for length in sz.lengths],
        info, place, late, t2, own, got, (first, second), acc, lf, spread, begun,
    )


def solution(mesh):
    in_specs = (P("row", "col"), P("row", "col"), P("row", "col"), P("row", "col"))
    return jax.shard_map(
        functools.partial(body, mesh.shape["row"], mesh.shape["col"]),
        mesh=mesh,
        in_specs=in_specs,
        out_specs=P("row", "col"),
        check_vma=False,
    )
```

```python
import functools

import jax
import jax.numpy as jnp
from jax import lax
from jax.experimental import pallas as pl
from jax.experimental.pallas import tpu as pltpu
from jax.sharding import PartitionSpec as P

TILE = 128
PAIR = 2 * TILE
NOTE = 16
BF16 = jnp.bfloat16
LEFTS = 6
SMEM = pl.BlockSpec(memory_space=pltpu.SMEM)
VMEM = pl.BlockSpec(memory_space=pltpu.VMEM)
ANY = pl.BlockSpec(memory_space=pl.ANY)
HBM = pl.BlockSpec(memory_space=pltpu.HBM)
PARAMS = pltpu.CompilerParams(vmem_limit_bytes=40 << 20)
COST = pl.CostEstimate(flops=1 << 20, bytes_accessed=1 << 12, transcendentals=0)
LENGTHS = (8, 10, 12, 14, 16, 20)
FIRST = 24


def rows(tile, count=1):
    return pl.ds(pl.multiple_of(tile * TILE, TILE), count * TILE)


def tiles(count):
    return jax.ShapeDtypeStruct((count * TILE, TILE), BF16)


class Sizes:
    def __init__(self, n, k_tiles, n_tiles):
        self.n, self.kd, self.nd = n, k_tiles, n_tiles
        self.all = k_tiles * n_tiles
        self.main = self.all * 3 // 4
        self.first = self.main * FIRST // 48
        self.left = self.all - self.main
        self.stream = (n - 1) * self.left
        self.pairs = n_tiles // 2
        self.near = n // 2
        self.sure = (self.main // k_tiles) // 2
        lengths = {-(-f * self.stream // 48) for f in LENGTHS}
        self.lengths = sorted(lengths | {self.stream})

    def cut(self, c):
        start, stop = ((0, self.first), (self.first, self.main))[c]
        begin = NOTE + start * TILE if c else 0
        return start, stop - start, pl.ds(begin, NOTE + stop * TILE - begin)


def begin_kernel(
    sz, mask_v, v_mask_hbm, t2_mask_hbm, v, t2, main, lf, t2_out,
    v_v, t2_v, packed, v_mask, t2_mask, note, v_sem, sem,
):
    group = sz.nd // v_sem.shape[0]
    copies = []
    for g in range(v_sem.shape[0]):
        at = pl.ds(g * group * TILE, group * TILE)
        copies.append(pltpu.make_async_copy(v.at[:, at], v_v.at[:, at], v_sem.at[g]))
    mask_copy = pltpu.make_async_copy(v_mask_hbm, v_mask, sem.at[0])
    t2_copies = (
        pltpu.make_async_copy(t2_mask_hbm, t2_mask, sem.at[1]),
        pltpu.make_async_copy(t2, t2_v, sem.at[2]),
    )
    for copy in (mask_copy, *copies, *t2_copies):
        copy.start()
    note[...] = jnp.zeros_like(note)
    note[: sz.kd, : sz.nd] = (mask_v[...] > 0).astype(jnp.int32)
    mask_copy.wait()
    pos = jnp.int32(0)
    for c in range(sz.nd):
        if c % group == 0:
            copies[c // group].wait()
        for k in range(sz.kd):
            packed[rows(pos), :] = v_v[k * TILE : (k + 1) * TILE, c * TILE : (c + 1) * TILE]
            pos = pos + (v_mask[k, c] > 0).astype(jnp.int32)
    main[:NOTE, :] = note[...].astype(BF16)
    main[NOTE:, :] = packed[: sz.main * TILE, :]
    lf[...] = packed[sz.main * TILE :, :]
    for copy in t2_copies:
        copy.wait()
    for k in range(t2_mask.shape[0]):
        for i in range(t2_mask.shape[1]):
            at = (slice(i * TILE, (i + 1) * TILE), slice(k * TILE, (k + 1) * TILE))
            tile = t2_v[at]
            t2_out[at] = jnp.where(t2_mask[k, i] > 0, tile, jnp.zeros_like(tile))


def begin(sz, v, t2, v_mask, t2_mask):
    groups = 4 if sz.nd % 4 == 0 else 1
    return pl.pallas_call(
        functools.partial(begin_kernel, sz),
        out_shape=(
            jax.ShapeDtypeStruct((NOTE + sz.main * TILE, TILE), BF16),
            tiles(sz.left),
            jax.ShapeDtypeStruct(t2.shape, BF16),
        ),
        in_specs=[VMEM, HBM, HBM, HBM, HBM],
        out_specs=(VMEM, VMEM, VMEM),
        scratch_shapes=[
            pltpu.VMEM(v.shape, BF16),
            pltpu.VMEM(t2.shape, BF16),
            pltpu.VMEM((sz.all * TILE, TILE), BF16),
            pltpu.SMEM(v_mask.shape, jnp.int32),
            pltpu.SMEM(t2_mask.shape[::-1], jnp.int32),
            pltpu.VMEM((NOTE, TILE), jnp.int32),
            pltpu.SemaphoreType.DMA((groups,)),
            pltpu.SemaphoreType.DMA((3,)),
        ],
        compiler_params=pltpu.CompilerParams(vmem_limit_bytes=60 << 20),
        name="begin",
    )(v_mask, v_mask, t2_mask.T, v, t2)


def need_kernel(sz, here, *refs):
    n = sz.n
    parts, (out, notes, sem) = refs[: 2 * n - 3], refs[2 * n - 3 :]
    copies = [
        pltpu.make_async_copy(ref.at[pl.ds(0, NOTE), :], notes.at[i], sem.at[i])
        for i, ref in enumerate(parts)
    ]
    for copy in copies:
        copy.start()
    for copy in copies:
        copy.wait()
    me = here[0]
    sources = [me]
    for s in range(n - 2):
        sources += [me - 1 - s, me + 1 + s]
    to_up = to_down = jnp.int32(0)
    for i, z in enumerate(sources):
        count = jnp.sum(notes[i].astype(jnp.float32)).astype(jnp.int32)
        left = jnp.where(jnp.logical_and(z >= 0, z < n), jnp.maximum(count - sz.main, 0), 0)
        to_up = to_up + jnp.where(z == n - 1, 0, left)
        to_down = to_down + jnp.where(z == 0, 0, left)
    out[0] = jnp.maximum(to_up, to_down)


def from_source(sz, me, own, got, act, take=None):
    for m in range(sz.n):

        @pl.when(me == m)
        def _():
            for z in range(sz.n):
                if take is None or take(m, z):
                    act(z, own if z == m else got[abs(z - m) - 1][0 if z < m else 1])


def near_plan_kernel(sz, here, own, *refs):
    h = sz.near
    parts, (place, notes, wide, masks, note_sem, mask_sem) = refs[: 2 * h - 2], refs[2 * h - 2 :]

    def note_copy(z, ref):
        at = ref.at[pl.ds(0, NOTE), :]
        return pltpu.make_async_copy(at, notes.at[pl.ds(z % h * NOTE, NOTE), :], note_sem.at[z % h])

    got = [parts[2 * s : 2 * s + 2] for s in range(h - 1)]
    from_source(sz, here[0], own, got, lambda z, ref: note_copy(z, ref).start(), lambda m, z: m // h == z // h)
    for z in range(h):
        note_copy(z, own).wait()
    wide[...] = notes[...].astype(jnp.int32)
    mask_copy = pltpu.make_async_copy(wide, masks, mask_sem)
    mask_copy.start()
    mask_copy.wait()

    def column(c, counts):
        counts = list(counts)
        keeps = [[masks[z * NOTE + k, c] > 0 for k in range(sz.kd)] for z in range(h)]
        for z in range(h):
            for k in range(sz.kd):
                kept, p = keeps[z][k], counts[z]
                at = jnp.where(jnp.logical_and(kept, p < sz.main), z * sz.main + p, h * sz.main)
                place[(c * h + z) * sz.kd + k] = at
                counts[z] = p + kept.astype(jnp.int32)
        return tuple(counts)

    lax.fori_loop(0, 2 * sz.sure, column, (jnp.int32(0),) * h)


def near_plan(sz, here, own, got):
    h, ops = sz.near, (own, *(part for hop in got for part in hop))
    return pl.pallas_call(
        functools.partial(near_plan_kernel, sz),
        out_shape=jax.ShapeDtypeStruct((2 * sz.sure * h * sz.kd,), jnp.int32),
        in_specs=[SMEM] + [ANY] * len(ops),
        out_specs=SMEM,
        scratch_shapes=[
            pltpu.VMEM((h * NOTE, TILE), BF16),
            pltpu.VMEM((h * NOTE, TILE), jnp.int32),
            pltpu.SMEM((h * NOTE, TILE), jnp.int32),
            pltpu.SemaphoreType.DMA((h,)),
            pltpu.SemaphoreType.DMA,
        ],
        name="near_plan",
    )(here, *ops)


def plan_kernel(sz, here, *refs):
    n, me = sz.n, here[0]
    own, *parts, end = refs[: 2 * n - 2]
    place, late, info, notes, wide, masks, note_sem, mask_sem = refs[2 * n - 2 :]

    def note_copy(z, ref):
        at = ref.at[pl.ds(0, NOTE), :]
        return pltpu.make_async_copy(at, notes.at[pl.ds(z * NOTE, NOTE), :], note_sem.at[z])

    got = [parts[2 * s : 2 * s + 2] for s in range(n - 2)] + [(end, end)]
    from_source(sz, me, own, got, lambda z, ref: note_copy(z, ref).start())
    for z in range(n):
        note_copy(z, own).wait()
    wide[...] = notes[...].astype(jnp.int32)
    mask_copy = pltpu.make_async_copy(wide, masks, mask_sem)
    mask_copy.start()
    mask_copy.wait()

    def column(c, carry):
        counts, firsts, seconds = (list(carry[i * n : (i + 1) * n]) for i in range(3))
        keeps = [[masks[z * NOTE + k, c] > 0 for k in range(sz.kd)] for z in range(n)]
        for z in range(n):
            have = jnp.where(me == z, sz.all, sz.main)
            for k in range(sz.kd):
                i = c * n * sz.kd + z * sz.kd + k
                kept, p = keeps[z][k], counts[z]
                place[i] = jnp.where(jnp.logical_and(kept, p < have), z * sz.all + p, n * sz.all)
                late[i] = jnp.where(jnp.logical_and(kept, p >= have), p - sz.main, -1)
                counts[z] = p + kept.astype(jnp.int32)
            firsts[z] = jnp.minimum(firsts[z], jnp.where(counts[z] > sz.first, c, sz.nd))
            seconds[z] = jnp.minimum(seconds[z], jnp.where(counts[z] > have, c, sz.nd))
        return tuple(counts + firsts + seconds)

    start = (jnp.int32(0),) * n + (jnp.int32(sz.nd),) * (2 * n)
    out = lax.fori_loop(0, sz.nd, column, start)
    lefts = [jnp.maximum(c - sz.main, 0) for c in out[:n]]
    info[0] = me
    info[1] = jnp.int32(0)
    info[2] = functools.reduce(jnp.minimum, out[n : 2 * n], jnp.int32(2 * sz.sure)) // 2
    info[3] = functools.reduce(jnp.minimum, out[2 * n :], jnp.int32(sz.nd - 2)) // 2
    info[4] = jnp.int32(sz.pairs)
    info[5] = here[1]
    for z in range(n):
        info[LEFTS + z] = lefts[z]


def plan(sz, here, own, got, end):
    n, ops = sz.n, (own, *(part for hop in got for part in hop), end)
    return pl.pallas_call(
        functools.partial(plan_kernel, sz),
        out_shape=(
            jax.ShapeDtypeStruct((sz.n * sz.all,), jnp.int32),
            jax.ShapeDtypeStruct((sz.n * sz.all,), jnp.int32),
            jax.ShapeDtypeStruct((LEFTS + sz.n,), jnp.int32),
        ),
        in_specs=[SMEM] + [ANY] * len(ops),
        out_specs=(SMEM, SMEM, SMEM),
        scratch_shapes=[
            pltpu.VMEM((n * NOTE, TILE), BF16),
            pltpu.VMEM((n * NOTE, TILE), jnp.int32),
            pltpu.SMEM((n * NOTE, TILE), jnp.int32),
            pltpu.SemaphoreType.DMA((n,)),
            pltpu.SemaphoreType.DMA,
        ],
        name="plan",
    )(here, *ops)


def choose_kernel(sz, c, here, need, up, down, out, sem):
    at = sz.cut(c)[2]
    size = out.shape[0] - at.size
    if size:
        out[:size, :] = jnp.full((size, TILE), need[0].astype(jnp.float32)).astype(BF16)
    for mine, x in ((here[0] == sz.n - 2, up), (here[0] != sz.n - 2, down)):

        @pl.when(mine)
        def _():
            copy = pltpu.make_async_copy(x.at[at, :], out.at[pl.ds(size, at.size), :], sem)
            copy.start()
            copy.wait()


def choose(sz, c, here, need, up, down):
    return pl.pallas_call(
        functools.partial(choose_kernel, sz, c),
        out_shape=jax.ShapeDtypeStruct((sz.cut(c)[2].size + c * NOTE, TILE), BF16),
        in_specs=[SMEM, SMEM, ANY, ANY],
        out_specs=VMEM,
        scratch_shapes=[pltpu.SemaphoreType.DMA],
        compiler_params=PARAMS,
        name="choose",
    )(here, need, up, down)


def first_kernel(sz, here, *refs):
    parts, (out, need, notes, note_sem, sem) = refs[: 2 * sz.n - 3], refs[2 * sz.n - 3 :]
    at = sz.cut(0)[2]
    up, down = (pltpu.make_async_copy(x.at[at, :], out, sem) for x in parts[-2:])
    mine = here[0] == sz.n - 2
    pl.when(mine)(lambda: up.start())
    pl.when(jnp.logical_not(mine))(lambda: down.start())
    need_kernel(sz, here, *parts, need, notes, note_sem)
    up.wait()


def choose_first(sz, here, own, got):
    ops = (own, *(part for hop in got for part in hop))
    return pl.pallas_call(
        functools.partial(first_kernel, sz),
        out_shape=(
            jax.ShapeDtypeStruct((sz.cut(0)[2].size, TILE), BF16),
            jax.ShapeDtypeStruct((1,), jnp.int32),
        ),
        in_specs=[SMEM] + [ANY] * len(ops),
        out_specs=(VMEM, SMEM),
        scratch_shapes=[
            pltpu.VMEM((len(ops), NOTE, TILE), BF16),
            pltpu.SemaphoreType.DMA((len(ops),)),
            pltpu.SemaphoreType.DMA,
        ],
        compiler_params=PARAMS,
        name="choose_first",
    )(here, *ops)


def pool_kernel(sz, length, info, lf, *refs):
    n, me = sz.n, info[0]
    spread, (out, joined) = refs[: n - 1], refs[n - 1 :]
    for source, order in ((n - 2, range(n - 2, -1, -1)), (1, range(1, n))):

        @pl.when(me == source)
        def _():
            at = jnp.int32(0)
            for z in order:
                part = lf if z == source else spread[(z ^ source) - 1]
                joined[rows(at, sz.left), :] = part[...]
                at = at + info[LEFTS + z]
            out[...] = joined[: length * TILE, :]


def pool(sz, length, info, lf, spread):
    return pl.pallas_call(
        functools.partial(pool_kernel, sz, length),
        out_shape=tiles(length),
        in_specs=[SMEM] + [VMEM] * sz.n,
        out_specs=VMEM,
        scratch_shapes=[pltpu.VMEM((sz.stream * TILE, TILE), BF16)],
        compiler_params=PARAMS,
        name="pool",
    )(info, lf, *spread)


def out_copy(out, held, sem, slot, pair, r):
    half = held.shape[1] // 2
    at = pl.ds(pl.multiple_of(r * half, half), half)
    if len(out.shape) == 3:
        to = out.at[pair, at, :]
    else:
        to = out.at[at, pl.ds(pl.multiple_of(pair * PAIR, PAIR), PAIR)]
    return pltpu.make_async_copy(held.at[slot, at, :], to, sem.at[slot, r])


def t2_copies(act, col, part, t2, t2_v, sem, rs=(0, 1)):
    half, wide, nh = t2_v.shape[0] // 2, t2_v.shape[1] // len(t2), len(t2) // 2
    mine = col // nh == part
    for which, ds in ((mine, range(nh)), (jnp.logical_not(mine), range(nh, 2 * nh))):

        @pl.when(which)
        def _():
            for r in rs:
                at = pl.ds(pl.multiple_of(r * half, half), half)
                for d in ds:
                    to = t2_v.at[at, pl.ds(pl.multiple_of((col ^ d) * wide, wide), wide)]
                    act(pltpu.make_async_copy(t2[d].at[at, :], to, sem.at[d, r]))


def start(copy):
    copy.start()


def wait(copy):
    copy.wait()


def multiply(lo, hi, build, t2_wait, t2_v, out, held, sem, span=slice(None), acc=None, acc_v=None, acc_sem=None):
    half = held.shape[1] // 2

    def acc_copy(pair, slot):
        return pltpu.make_async_copy(acc.at[pair], acc_v.at[slot], acc_sem.at[slot, 0])

    if acc is not None:

        @pl.when(lo < hi)
        def _():
            acc_copy(lo, 0).start()

    @pl.when(lo >= hi)
    def _():
        t2_wait((0, 1))

    @pl.loop(lo, hi)
    def _(pair):
        slot = lax.rem(pair - lo, 2)
        b = build(pair)
        if acc is not None:

            @pl.when(pair + 1 < hi)
            def _():
                acc_copy(pair + 1, 1 - slot).start()

            acc_copy(pair, slot).wait()

        @pl.when(pair >= lo + 2)
        def _():
            for r in range(2):
                out_copy(out, held, sem, slot, pair, r).wait()

        @pl.loop(0, 2)
        def _(r):
            @pl.when(pair == lo)
            def _():
                t2_wait((r,))

            at = pl.ds(pl.multiple_of(r * half, half), half)
            product = jnp.dot(t2_v[at, span], b[...], preferred_element_type=jnp.float32)
            if acc is not None:
                product = product + acc_v[slot, at, :]
            held[slot, at, :] = product.astype(held.dtype)
            out_copy(out, held, sem, slot, pair, r).start()

    for back in (1, 2):

        @pl.when(hi - back >= lo)
        def _():
            for r in range(2):
                out_copy(out, held, sem, lax.rem(hi - back - lo, 2), 0, r).wait()


def main_kernel(sz, chunks, n_t2, info, place, *refs):
    n = sz.n
    t2, refs = refs[:n_t2], refs[n_t2:]
    own, refs = refs[0], refs[1:]
    got, refs = [refs[2 * s : 2 * s + 2] for s in range(n - 2)], refs[2 * (n - 2) :]
    ends, refs = refs[:chunks], refs[chunks:]
    if chunks == 2:
        lf, acc, begun, out, rest, t2_v, packed, b, held, acc_v, in_sem, out_sem, acc_sem, t2_sem = refs
    else:
        acc, out, packed, b, held, acc_v, t2_v, in_sem, out_sem, acc_sem, t2_sem = refs
    me, col, h = info[0], info[5], sz.near
    far = jnp.where(me < h, h, 0)

    def chunk_copy(ref, z, c):
        start, count, at = sz.cut(c)
        size = count * TILE
        first = at.start + at.size - size if ref.shape[0] == NOTE + sz.main * TILE else ref.shape[0] - size
        to = packed.at[pl.ds((z * sz.all + start) * TILE, size), :]
        return pltpu.make_async_copy(ref.at[pl.ds(first, size), :], to, in_sem.at[z, c])

    def start_chunks(take):
        for c in range(chunks):
            parts = got + [(ends[c], ends[c])]
            from_source(sz, me, own, parts, lambda z, ref: chunk_copy(ref, z, c).start(), take)

    def wait_chunks(first):
        for i in range(h):
            for c in range(chunks):
                chunk_copy(own, first + i, c).wait()

    def t2_part(act, part, rs):
        t2_copies(act, col, part, t2, t2_v, t2_sem, rs)

    far_part = far // h
    start_chunks(lambda m, z: m // h != z // h)
    t2_part(start, far_part, (0, 1))
    if chunks == 2:
        start_chunks(lambda m, z: m // h == z // h)
        t2_part(start, 1 - far_part, (0, 1))
        left_copy = pltpu.make_async_copy(
            lf, packed.at[rows(me * sz.all + sz.main, sz.left), :], in_sem.at[0, 2]
        )
        left_copy.start()
    packed[n * sz.all * TILE :, :] = jnp.zeros((TILE, TILE), BF16)
    wait_chunks(far)

    def build(pair, to, first, count):
        @pl.loop(0, count * sz.kd)
        def _(k):
            for c in range(2):
                tile = packed[rows(place[((2 * pair + c) * n + first) * sz.kd + k]), :]
                to[rows(k), c * TILE : (c + 1) * TILE] = tile

        return to

    deep = h * sz.kd * TILE
    multiply(
        info[chunks], jnp.minimum(info[chunks + 1], sz.sure),
        lambda pair: build(pair, b.at[pl.ds(0, deep), :], far, h),
        lambda rs: t2_part(wait, far_part, rs), t2_v, out, held, out_sem,
        pl.ds(pl.multiple_of(far * sz.kd * TILE, deep), deep), acc, acc_v, acc_sem,
    )
    if chunks == 2:
        wait_chunks(h - far)
        left_copy.wait()
        t2_part(wait, 1 - far_part, (0, 1))
        multiply(
            jnp.int32(sz.sure), info[3], lambda pair: build(pair, b, 0, n),
            lambda rs: None, t2_v, out, held, out_sem,
        )
        for j in range(sz.pairs - sz.sure):

            @pl.when(sz.sure + j >= info[3])
            def _():
                build(sz.sure + j, rest.at[j], 0, n)


def early_kernel(sz, n_t2, here, place, *refs):
    h = sz.near
    t2, own, refs = refs[:n_t2], refs[n_t2], refs[n_t2 + 1 :]
    got, refs = [refs[2 * s : 2 * s + 2] for s in range(h - 1)], refs[2 * (h - 1) :]
    acc, packed, b, held, t2_v, in_sem, out_sem, t2_sem = refs
    me, col = here[0], here[1]

    def main_copy(ref, z):
        to = packed.at[pl.ds(z % h * sz.main * TILE, sz.main * TILE), :]
        return pltpu.make_async_copy(ref.at[pl.ds(NOTE, sz.main * TILE), :], to, in_sem.at[z % h])

    from_source(sz, me, own, got, lambda z, ref: main_copy(ref, z).start(), lambda m, z: m // h == z // h)
    part = me // h
    t2_copies(start, col, part, t2, t2_v, t2_sem)
    packed[h * sz.main * TILE :, :] = jnp.zeros((TILE, TILE), BF16)
    for z in range(h):
        main_copy(own, z).wait()

    def build(pair):
        @pl.loop(0, h * sz.kd)
        def _(k):
            for c in range(2):
                tile = packed[rows(place[(2 * pair + c) * h * sz.kd + k]), :]
                b[rows(k), c * TILE : (c + 1) * TILE] = tile

        return b

    deep = h * sz.kd * TILE
    span = pl.ds(pl.multiple_of(jnp.where(me < h, 0, deep), deep), deep)
    multiply(
        jnp.int32(0), jnp.int32(sz.sure), build,
        lambda rs: t2_copies(wait, col, part, t2, t2_v, t2_sem, rs), t2_v, acc, held, out_sem, span,
    )


def early_part(sz, here, place, t2, own, got):
    ij, cd = t2[0].shape[0], t2[0].shape[1] * len(t2)
    ops = [*t2, own, *(part for hop in got for part in hop)]
    return pl.pallas_call(
        functools.partial(early_kernel, sz, len(t2)),
        out_shape=pltpu.HBM((sz.sure, ij, PAIR), jnp.float32),
        in_specs=[SMEM, SMEM] + [ANY] * len(ops),
        out_specs=HBM,
        scratch_shapes=[
            pltpu.VMEM(((sz.near * sz.main + 1) * TILE, TILE), BF16),
            pltpu.VMEM((cd // 2, PAIR), BF16),
            pltpu.VMEM((2, ij, PAIR), jnp.float32),
            pltpu.VMEM((ij, cd), BF16),
            pltpu.SemaphoreType.DMA((sz.near,)),
            pltpu.SemaphoreType.DMA((2, 2)),
            pltpu.SemaphoreType.DMA((len(t2), 2)),
        ],
        compiler_params=PARAMS,
        cost_estimate=COST,
        name="early_part",
    )(here, place, *ops)


def main_part(sz, chunks, info, place, t2, own, got, ends, acc, lf=None, begun=None):
    ij, cd = t2[0].shape[0], t2[0].shape[1] * len(t2)
    ops = [*t2, own, *(part for hop in got for part in hop), *ends[:chunks]]
    out_shape = [pltpu.HBM((ij, sz.nd * TILE), BF16)]
    aliases = {}
    if chunks == 2:
        ops += [lf, acc, begun]
        aliases = {2 + len(ops) - 1: 0}
        out_shape.append(jax.ShapeDtypeStruct((sz.pairs - sz.sure, cd, PAIR), BF16))
        out_shape.append(pltpu.VMEM((ij, cd), BF16))
    else:
        ops += [acc]
    out = pl.pallas_call(
        functools.partial(main_kernel, sz, chunks, len(t2)),
        out_shape=out_shape,
        in_specs=[SMEM, SMEM] + [ANY] * len(ops),
        out_specs=[HBM, VMEM, VMEM][: 2 * chunks - 1],
        scratch_shapes=[
            pltpu.VMEM(((sz.n * sz.all + 1) * TILE, TILE), BF16),
            pltpu.VMEM((cd, PAIR), BF16),
            pltpu.VMEM((2, ij, PAIR), BF16),
            pltpu.VMEM((2, ij, PAIR), jnp.float32),
            *([pltpu.VMEM((ij, cd), BF16)] if chunks == 1 else []),
            pltpu.SemaphoreType.DMA((sz.n, 3)),
            pltpu.SemaphoreType.DMA((2, 2)),
            pltpu.SemaphoreType.DMA((2, 2)),
            pltpu.SemaphoreType.DMA((len(t2), 2)),
        ],
        input_output_aliases=aliases,
        compiler_params=PARAMS,
        cost_estimate=COST,
        name="main_part",
    )(info, place, *ops)
    return out if chunks == 2 else out[0]


def tail_kernel(sz, info, late, begun, rest, t2_v, end, *refs):
    n, me, whole = sz.n, info[0], info[3]
    spread, (out, b, extra, held, in_sem, out_sem) = refs[: n - 1], refs[n - 1 :]
    is_end = jnp.logical_or(me == 0, me == n - 1)
    size = sz.left * TILE
    from_pool = [pltpu.make_async_copy(end, extra.at[pl.ds(0, end.shape[0]), :], in_sem.at[0])]
    direct = [
        pltpu.make_async_copy(part, extra.at[pl.ds(i * size, size), :], in_sem.at[i])
        for i, part in enumerate(spread)
    ]

    def each(act):
        for which, copies in ((is_end, from_pool), (jnp.logical_not(is_end), direct)):

            @pl.when(which)
            def _():
                for copy in copies:
                    act(copy)

    each(lambda copy: copy.start())
    for j in range(sz.pairs - sz.sure):

        @pl.when(sz.sure + j >= whole)
        def _():
            b[j] = rest[j]

    bases = []
    for z in range(n):
        top = sum((info[LEFTS + y] for y in range(z + 1, n - 1)), jnp.int32(0))
        bottom = sum((info[LEFTS + y] for y in range(1, z)), jnp.int32(0))
        base = jnp.where(is_end, jnp.where(me == 0, bottom, top), ((me ^ z) - 1) * sz.left)
        bases.append(base)

    each(lambda copy: copy.wait())
    for j in range(sz.pairs - sz.sure):

        @pl.when(sz.sure + j >= whole)
        def _():
            for z in range(n):

                @pl.loop(0, sz.kd)
                def _(k):
                    for c in range(2):
                        p = late[((2 * (sz.sure + j) + c) * n + z) * sz.kd + k]

                        @pl.when(p >= 0)
                        def _():
                            b[j, rows(z * sz.kd + k), c * TILE : (c + 1) * TILE] = extra[
                                rows(bases[z] + p), :
                            ]

    multiply(whole, info[4], lambda pair: b.at[pair - sz.sure], lambda rs: None, t2_v, out, held, out_sem)


def tail_part(sz, info, late, t2_v, begun, rest, end, spread):
    ij, cd = t2_v.shape
    pairs = sz.pairs - sz.sure
    region = max(end.shape[0], (sz.n - 1) * sz.left * TILE)
    return pl.pallas_call(
        functools.partial(tail_kernel, sz),
        out_shape=pltpu.HBM(begun.shape, BF16),
        in_specs=[SMEM, SMEM, HBM, VMEM, VMEM] + [ANY] * sz.n,
        out_specs=HBM,
        scratch_shapes=[
            pltpu.VMEM((pairs, cd, PAIR), BF16),
            pltpu.VMEM((region, TILE), BF16),
            pltpu.VMEM((2, ij, PAIR), BF16),
            pltpu.SemaphoreType.DMA((sz.n - 1,)),
            pltpu.SemaphoreType.DMA((2, 2)),
        ],
        input_output_aliases={2: 0},
        compiler_params=PARAMS,
        cost_estimate=COST,
        name="tail_part",
    )(info, late, begun, rest, t2_v, end, *spread)


def last_hop(sz, length, info, place, late, t2, own, got, ends, acc, lf, spread, begun):
    n = sz.n
    came = lax.ppermute(pool(sz, length, info, lf, spread), "row", [(n - 2, n - 1), (1, 0)])
    begun, rest, t2_v = main_part(sz, 2, info, place, t2, own, got, ends, acc, lf, begun)
    return tail_part(sz, info, late, t2_v, begun, rest, came, spread)


def tie(value, after):
    return lax.optimization_barrier((value, after))[0]


def body(n, n_col, t2_amps, v_ints, t2_mask, v_mask):
    sz = Sizes(n, *v_mask.shape)
    me = lax.axis_index("row")
    here = jnp.stack([me, lax.axis_index("col")])
    own, lf, screened = begin(sz, v_ints, t2_amps, v_mask, t2_mask)

    def hop(s, value, after=None):
        up, down = value
        if after is not None:
            up, down = tie(up, after), tie(down, after)
        pairs = [(i, i + 1) for i in range(s, n - 1)]
        back = [(n - 1 - i, n - 1 - j) for i, j in pairs]
        return lax.ppermute(up, "row", pairs), lax.ppermute(down, "row", back)

    def across(value, d):
        return lax.ppermute(value, "col", [(i, i ^ d) for i in range(n_col)])

    t2 = {0: screened}
    got = [hop(0, (own, own))]
    for d in range(2, n_col, 2):
        t2[d] = across(screened if d < 6 else tie(screened, t2[2]), d)
    for s in range(1, n - 2):
        got.append(hop(s, got[-1], (t2[2], t2[4]) if s == 1 else None))
    near = got[: sz.near - 1]
    near_place = near_plan(sz, here, own, near)
    for d in range(0, n_col, 2):
        t2[d + 1] = across(tie(t2[d], near_place) if d == 4 else t2[d], 1)
    t2 = [t2[d] for d in range(n_col)]
    ends = [(n - 2, n - 1), (1, 0)]

    def leftovers(d, after):
        pairs = [(i, i ^ d) for i in range(n) if 0 < i ^ d < n - 1]
        return lax.ppermute(tie(lf, after), "row", pairs)

    spread = {1: leftovers(1, got[0])}
    acc = early_part(sz, here, near_place, t2, own, near)
    first, need = choose_first(sz, tie(here, (t2, spread[1], acc)), own, got)
    first = lax.ppermute(first, "row", ends)
    need = lax.pmax(need, "col")
    second = lax.ppermute(choose(sz, 1, here, need, *got[-1]), "row", ends)
    spread.update({d: leftovers(d, need) for d in range(2, n)})
    spread = [spread[d] for d in range(1, n)]
    place, late, info = plan(sz, tie(here, need), own, got, first)
    begun = main_part(sz, 1, info, place, t2, own, got, (first,), acc)
    is_end = jnp.logical_or(me == 0, me == n - 1)
    need = jnp.where(is_end, tie(second, begun)[0, 0].astype(jnp.int32), need[0])

    branch = sum((need > length).astype(jnp.int32) for length in sz.lengths[:-1])
    return lax.switch(
        branch,
        [functools.partial(last_hop, sz, length) for length in sz.lengths],
        info, place, late, t2, own, got, (first, second), acc, lf, spread, begun,
    )


def solution(mesh):
    in_specs = (P("row", "col"), P("row", "col"), P("row", "col"), P("row", "col"))
    return jax.shard_map(
        functools.partial(body, mesh.shape["row"], mesh.shape["col"]),
        mesh=mesh,
        in_specs=in_specs,
        out_specs=P("row", "col"),
        check_vma=False,
    )
```
